32 devices in a mesh: blk: 8 (over z, x), dp: 4 (over y, core).
Axes of the slice: x: 2, y: 2, z: 4, core: 2. Of those that a mesh axis runs over, the one named last changes fastest.
Arguments:
- tokens: bfloat16 [4, 1024, 1472], P('dp', 'blk'), may hold values from -6 to 6
- lengths: int32 [4, 8], P('dp'), may hold values from 1 to 1024, as said below
- bucket_table: int32 [257], replicated, may hold values from 0 to 31
- first_gain: bfloat16 [1472], replicated, may hold values from 0.5 to 1.5
- position_bias: bfloat16 [32, 6], replicated, may hold values from -4 to 4
- w_query: bfloat16 [1472, 384], replicated, may hold values from -0.02734375 to 0.02734375
- w_key: bfloat16 [1472, 384], replicated, may hold values from -0.15625 to 0.15625
- w_value: bfloat16 [1472, 384], replicated, may hold values from -0.15625 to 0.15625
- w_output: bfloat16 [384, 1472], replicated, may hold values from -3 to 3
- second_gain: bfloat16 [1472], replicated, may hold values from 0.5 to 1.5
- w_gate: bfloat16 [1472, 3584], replicated, may hold values from -0.15625 to 0.15625
- w_up: bfloat16 [1472, 3584], replicated, may hold values from -0.15625 to 0.15625
- w_down: bfloat16 [3584, 1472], replicated, may hold values from -0.1875 to 0.1875
- cotangent: bfloat16 [4, 1024, 1472], P('dp', 'blk'), may hold values from -6 to 6
Outputs:
- mixed: bfloat16 [4, 1024, 1472], P('dp', 'blk')
- tokens_gradient: float32 [4, 1024, 1472], P('dp', 'blk')
- first_gain_gradient: float32 [1472], replicated
- position_bias_gradient: float32 [32, 6], replicated
- query_gradient: float32 [1472, 384], P(None, 'blk')
- key_gradient: float32 [1472, 384], P(None, 'blk')
- value_gradient: float32 [1472, 384], P(None, 'blk')
- output_gradient: float32 [384, 1472], P('blk')
- second_gain_gradient: float32 [1472], replicated
- gate_gradient: float32 [1472, 3584], P(None, ('blk', 'dp'))
- up_gradient: float32 [1472, 3584], P(None, ('blk', 'dp'))
- down_gradient: float32 [3584, 1472], P(('blk', 'dp'))
The draws below stay inside these ranges and needn't reach their ends.
Inputs may be any that keep to these rules, and one draw needn't show every extreme that they name: `lengths`: each row sums to 1024; in each row one item, at a place drawn from the seed, begins within the first 128 positions and ends within the last 128; every other item is at most 16 long.
All inputs are finite; a program needn't handle non-finite values.
Results may differ from the reference program's by a relative error of at most 0.023.
Values may be sent and summed in bfloat16 or wider, within the bound.
A program may use at most 256 MiB of HBM per device.

```python
import math
import jax
import jax.numpy as jnp
from jax import lax

D = 1472
HEADS = 6
HEAD = 64
FF = 3584
BUCKETS = 32
REACH = 128
TOK_DEV = 128
ITEMS = 8
INNER = 384
PACK = 1024
N_DP = 4


def draw_lengths(key, part):
    key = jax.random.fold_in(key, 11)
    first, second = jax.random.split(key)
    shorts = jax.random.randint(first, (N_DP, ITEMS - 1), 1, TOK_DEV // 8 + 1, dtype=jnp.int32)
    places = jax.random.randint(second, (N_DP, 1), 0, ITEMS, dtype=jnp.int32)
    slots = jnp.arange(ITEMS, dtype=jnp.int32)[None, :]
    source = jnp.clip(jnp.where(slots < places, slots, slots - 1), 0, ITEMS - 2)
    picked = jnp.take_along_axis(shorts, jnp.broadcast_to(source, (N_DP, ITEMS)), axis=1)
    longest = PACK - jnp.sum(shorts, axis=1, keepdims=True)
    return jnp.where(slots == places, longest, picked).astype(jnp.int32)


def draw_bucket_table(key, part):
    key = jax.random.fold_in(key, 23)
    breaks = jax.random.permutation(key, REACH - 8)[:7].astype(jnp.int32) + 9
    spots = jnp.arange(2 * REACH + 1, dtype=jnp.int32)
    distance = jnp.abs(spots - REACH)
    level = jnp.where(distance < 8, distance, 8 + jnp.sum((distance[:, None] >= breaks[None, :]).astype(jnp.int32), axis=1))
    return (level + 16 * (spots > REACH).astype(jnp.int32)).astype(jnp.int32)


def steps_of(rng, shape, cuts, smallest, largest):
    def one(axis_at, parts):
        draws = jax.random.uniform(jax.random.fold_in(jax.random.fold_in(rng, 6), axis_at), (parts,), jnp.float32, smallest / len(cuts), largest / len(cuts))
        return jnp.repeat(jnp.exp(draws), shape[axis_at] // parts).reshape((-1,) + (1,) * (len(shape) - axis_at - 1))

    level = one(*cuts[0])
    for cut in cuts[1:]:
        level = level * one(*cut)
    return level


def scatter_about(key, extent, width, reach, shards=(), kind=jnp.bfloat16):
    values = width * jax.random.normal(key, extent, jnp.float32)
    if shards:
        values = values * steps_of(key, extent, shards, -0.22, 0.18)
    return jnp.clip(values, -reach, reach).astype(kind)


def setup_inputs(seed: int = 0) -> dict:
    seeds = jax.random.split(jax.random.key(seed), 15)
    return {
        "tokens": scatter_about(seeds[0], (N_DP, PACK, D), 1.0, 6.0, ((0, 4), (1, 8))),
        "lengths": draw_lengths(jax.random.fold_in(seeds[14], 71), 0),
        "bucket_table": draw_bucket_table(jax.random.fold_in(seeds[14], 71), 0),
        "first_gain": jnp.clip(1.0 + 0.1 * jax.random.normal(seeds[3], (D,), jnp.float32), 0.5, 1.5).astype(jnp.bfloat16),
        "position_bias": scatter_about(seeds[4], (BUCKETS, HEADS), 1.0, 4.0),
        "w_query": scatter_about(seeds[5], (D, INNER), (32 * D) ** -0.5, 0.02734375),
        "w_key": scatter_about(seeds[6], (D, INNER), D ** -0.5, 0.15625),
        "w_value": scatter_about(seeds[7], (D, INNER), D ** -0.5, 0.15625),
        "w_output": scatter_about(seeds[8], (INNER, D), (HEAD // 16) ** -0.5, 3.0),
        "second_gain": jnp.clip(1.0 + 0.1 * jax.random.normal(seeds[9], (D,), jnp.float32), 0.5, 1.5).astype(jnp.bfloat16),
        "w_gate": scatter_about(seeds[10], (D, FF), D ** -0.5, 0.15625),
        "w_up": scatter_about(seeds[11], (D, FF), D ** -0.5, 0.15625),
        "w_down": scatter_about(seeds[12], (FF, D), (FF // 4) ** -0.5, 0.1875),
        "cotangent": scatter_about(seeds[13], (N_DP, PACK, D), 1.0, 6.0, ((0, 4), (1, 8))),
    }


@jax.custom_vjp
def low(v):
    return lax.optimization_barrier(v.astype(jnp.bfloat16)).astype(jnp.float32)

@jax.custom_vjp
def low_back(v):
    return v

def low_keep(v):
    return (low(v), None)

def low_pass(kept, grad):
    return (grad,)

def back_keep(v):
    return (v, None)

def back_low(kept, grad):
    return (low(grad),)
low.defvjp(low_keep, low_pass)
low_back.defvjp(back_keep, back_low)

def matmul(left, right):
    return jnp.dot(left, right, precision=lax.Precision.HIGHEST, preferred_element_type=jnp.float32)

def normalize(values, gain):
    return values * lax.rsqrt(lax.optimization_barrier(jnp.mean(values * values, axis=-1, keepdims=True)) + 1e-06) * gain

def gelu_tanh(values):
    return 0.5 * values * (1.0 + jnp.tanh(math.sqrt(2.0 / math.pi) * (values + 0.044715 * values * values * values)))

def forward(params, pack_tokens, pack_lengths, bucket_table):
    first_gain, position_bias, w_query, w_key, w_value, w_output, second_gain, w_gate, w_up, w_down = params
    length = pack_tokens.shape[0]
    positions = jnp.arange(length, dtype=jnp.int32)
    ends = jnp.cumsum(pack_lengths).astype(jnp.int32)
    items = lax.optimization_barrier(jnp.sum((positions[:, None] >= ends[None, :]).astype(jnp.int32), axis=1))
    onehot = (bucket_table[:, None] == jnp.arange(BUCKETS, dtype=jnp.int32)[None, :]).astype(jnp.float32)
    head_table = matmul(onehot, position_bias)
    normed_first = low(normalize(pack_tokens, first_gain))
    queries = low(low_back(matmul(normed_first, w_query))).reshape(length, HEADS, HEAD)
    keys = low(low_back(matmul(normed_first, w_key))).reshape(length, HEADS, HEAD)
    values = low(low_back(matmul(normed_first, w_value))).reshape(length, HEADS, HEAD)
    block = math.gcd(length, 512)
    count = length // block

    def attend(inputs):
        start, query_block = inputs
        query_pos = start + jnp.arange(block, dtype=jnp.int32)
        query_items = lax.dynamic_slice(items, (start,), (block,))
        offset = jnp.clip(positions[None, :] - query_pos[:, None], -REACH, REACH) + REACH
        bias = jnp.transpose(jnp.take(head_table, offset, axis=0), (2, 0, 1))
        scores = jnp.einsum('qhd,khd->hqk', query_block, keys, precision=lax.Precision.HIGHEST) + bias
        mask = query_items[:, None] == items[None, :]
        scores = low_back(jnp.where(mask[None], scores, -1e+30))
        highest = lax.optimization_barrier(jnp.max(scores, axis=-1, keepdims=True))
        expo = jnp.exp(scores - highest)
        probs = low(expo / lax.optimization_barrier(jnp.sum(expo, axis=-1, keepdims=True)))
        return jnp.einsum('hqk,khd->qhd', probs, values, precision=lax.Precision.HIGHEST)
    starts = jnp.arange(count, dtype=jnp.int32) * block
    attended = lax.map(jax.checkpoint(attend), (starts, queries.reshape(count, block, HEADS, HEAD)))
    attention = low(low_back(attended.reshape(length, INNER)))
    middle = pack_tokens + low_back(matmul(attention, w_output))
    normed_second = low(normalize(middle, second_gain))
    gate = low_back(matmul(normed_second, w_gate))
    up_part = low_back(matmul(normed_second, w_up))
    hidden = low(gelu_tanh(gate) * up_part)
    return middle + matmul(hidden, w_down)

def reference(tokens, lengths, bucket_table, first_gain, position_bias, w_query, w_key, w_value, w_output, second_gain, w_gate, w_up, w_down, cotangent):
    params = tuple((p.astype(jnp.float32) for p in (first_gain, position_bias, w_query, w_key, w_value, w_output, second_gain, w_gate, w_up, w_down)))

    def one_pack(carry, inputs):
        pack_tokens, pack_lengths, pack_cot = inputs
        result, pullback = jax.vjp(lambda prm, tok: forward(prm, tok, pack_lengths, bucket_table), params, pack_tokens.astype(jnp.float32))
        grads, token_grad = pullback(pack_cot.astype(jnp.float32))
        carry = jax.tree.map(jnp.add, carry, grads)
        return (carry, (result.astype(jnp.bfloat16), token_grad))
    initial = tuple((jnp.zeros_like(p) for p in params))
    totals, (mixed, tokens_gradient) = lax.scan(one_pack, initial, (tokens, lengths, cotangent))
    return (mixed, tokens_gradient, totals[0], totals[1], totals[2], totals[3], totals[4], totals[5], totals[6], totals[7], totals[8], totals[9])
```

```python
import functools
import math

import jax
import jax.numpy as jnp
from jax import lax
from jax.experimental import pallas as pl
from jax.experimental.pallas import tpu as pltpu
from jax.sharding import PartitionSpec as P

F32 = jnp.float32
BF16 = jnp.bfloat16
EPS = 1e-06
ROOT = math.sqrt(2.0 / math.pi)
HI = 4
LANES = 128


def nn(left, right):
    return lax.dot_general(left, right, (((1,), (0,)), ((), ())), preferred_element_type=F32)


def nt(left, right):
    return lax.dot_general(left, right, (((1,), (1,)), ((), ())), preferred_element_type=F32)


def tn(left, right):
    return lax.dot_general(left, right, (((0,), (0,)), ((), ())), preferred_element_type=F32)


def widen(value, lanes):
    return jnp.concatenate(
        [value, jnp.zeros((value.shape[0], lanes - value.shape[1]), value.dtype)], axis=1
    )


def activation(gate, up, hidden_slope):
    square = gate * gate
    bent = jnp.tanh(ROOT * gate * (1.0 + 0.044715 * square))
    half = 0.5 * (1.0 + bent)
    value = gate * half
    slope = half + 0.5 * gate * (1.0 - bent * bent) * (ROOT * (1.0 + 3.0 * 0.044715 * square))
    return (
        (value * up).astype(BF16),
        (hidden_slope * up * slope).astype(BF16),
        (hidden_slope * value).astype(BF16),
    )


def layer_kernel(
    n_blk,
    n_dp,
    lengths,
    bucket_table,
    first_gain,
    second_gain,
    bias_table,
    tokens_hbm,
    cot_hbm,
    wq_hbm,
    wk_hbm,
    wv_hbm,
    wo_hbm,
    wg_hbm,
    wu_hbm,
    wd_hbm,
    mixed_out,
    tokgrad_out,
    small_out,
    attn_out,
    ff_out,
    tok_t,
    cot_t,
    tok,
    wq,
    wk,
    wv,
    wo,
    k_all,
    v_all,
    q_all,
    s_all,
    totals,
    deltas,
    probs,
    dq_rows,
    gat,
    streams,
    held_w,
    slopes,
    middle,
    mixed_acc,
    second_acc,
    attended,
    swap_out,
    swap_in,
    ff_part,
    ff_r1,
    ff_r2,
    rows,
    acol,
    grads_t,
    at_part,
    at_first,
    at_recv,
    ag,
    small,
    small_blk,
    small_dp,
    tables,
    onehot,
    diag,
    lay,
    load_sem,
    stream_sem,
    swap_sem,
    k_send,
    k_recv,
    v_send,
    v_recv,
    q_send,
    q_recv,
    s_send,
    s_recv,
    lt_send,
    lt_recv,
    de_send,
    de_recv,
    gat_send,
    gat_recv,
    row_send,
    row_recv,
    col_send,
    col_recv,
    ff_send,
    ff_sem,
    at_send,
    at_sem,
    ag_send,
    ag_sem,
    sb_send,
    sb_sem,
    sd_send,
    sd_sem,
):
    n_lo = n_blk // HI
    local, width = tok.shape
    lanes = rows.shape[2]
    inner = wq.shape[1]
    pairs = inner // LANES
    heads = 2 * pairs
    keys = n_blk * local
    ff = wg_hbm.shape[1]
    chunk = streams.shape[3]
    slots = streams.shape[1]
    half_ff = ff // 2
    n_chunk = half_ff // chunk
    cut = ff // (n_blk * n_dp)
    n_near = HI // 2
    last_dp = n_dp - 1

    blk = lax.axis_index("blk")
    dp = lax.axis_index("dp")
    hi, lo = blk // n_lo, blk % n_lo
    row_y, core = dp // 2, dp % 2
    z_far, z_near = hi // 2, hi % 2
    own = z_far * 4 + dp

    def push(src, dst, send, recv, to_blk, to_dp):
        return pltpu.make_async_remote_copy(
            src_ref=src,
            dst_ref=dst,
            send_sem=send,
            recv_sem=recv,
            device_id={"blk": to_blk, "dp": to_dp},
            device_id_type=pl.DeviceIdType.MESH,
        )

    loads = [
        pltpu.make_async_copy(src, dst, load_sem.at[i])
        for i, (src, dst) in enumerate(
            (
                (tokens_hbm, tok_t),
                (wk_hbm, wk),
                (wv_hbm, wv),
                (wq_hbm, wq),
                (cot_hbm, cot_t),
                (wo_hbm, wo),
            )
        )
    ]
    for load in loads:
        load.start()
    feeds = (wg_hbm, wu_hbm, wd_hbm)
    wide = chunk
    picks = []
    def piece_begin(q):
        xl, zn = q // n_near, q % n_near
        column = (((z_far * n_near + zn) * n_lo + xl) * n_dp + dp) * cut
        return column, jnp.minimum(column // LANES * LANES, ff - wide)

    for q in range(n_lo * n_near):
        start = pl.multiple_of(piece_begin(q)[1], LANES)
        for i, src in enumerate(feeds):
            picks.append(
                pltpu.make_async_copy(
                    src.at[:, pl.ds(start, wide)], streams.at[i, q], stream_sem.at[i, q]
                )
            )
    barrier = pltpu.get_barrier_semaphore()
    partners = [((blk + o) % n_blk, dp) for o in range(1, n_blk)]
    partners += [(blk, (dp + o) % n_dp) for o in range(1, n_dp)]
    for to_blk, to_dp in partners:
        pl.semaphore_signal(
            barrier,
            inc=1,
            device_id={"blk": to_blk, "dp": to_dp},
            device_id_type=pl.DeviceIdType.MESH,
        )

    z_other, near_other, lo_other = 1 - z_far, 1 - z_near, 1 - lo

    def place(zf, zn, xl):
        return (zf * n_near + zn) * n_lo + xl

    class Gather:
        def __init__(self, buf, send, recv):
            self.buf, self.send, self.recv = buf, send, recv

        def one(self, k, slot, to_blk):
            ref = self.buf.at[slot]
            return push(ref, ref, self.send.at[k], self.recv.at[k], to_blk, dp)

        def far(self):
            return self.one(0, blk, place(z_other, z_near, lo))

        def near(self, a):
            slot = place(z_other if a else z_far, z_near, lo)
            return self.one(1 + a, slot, place(z_far, near_other, lo))

        def low(self, a, b):
            slot = place(z_other if a else z_far, near_other if b else z_near, lo)
            return self.one(3 + 2 * a + b, slot, place(z_far, z_near, lo_other))

        def start(self):
            self.far().start()
            self.near(0).start()
            self.low(0, 0).start()

        def step_near(self):
            self.near(0).wait_recv()
            self.low(0, 1).start()

        def step_far(self):
            self.far().wait_recv()
            self.near(1).start()
            self.low(1, 0).start()

        def step_last(self):
            self.near(1).wait_recv()
            self.low(1, 1).start()

        def finish(self):
            for a in range(2):
                for b in range(2):
                    self.low(a, b).wait_recv()

        def drain(self):
            self.far().wait_send()
            for a in range(2):
                self.near(a).wait_send()
                for b in range(2):
                    self.low(a, b).wait_send()

    k_ring = Gather(k_all, k_send, k_recv)
    v_ring = Gather(v_all, v_send, v_recv)
    q_ring = Gather(q_all, q_send, q_recv)
    s_ring = Gather(s_all, s_send, s_recv)

    eye = (
        lax.broadcasted_iota(jnp.int32, (local, local), 0)
        == lax.broadcasted_iota(jnp.int32, (local, local), 1)
    ).astype(BF16)
    gain1 = first_gain[...].astype(F32).reshape(1, width)
    gain2 = second_gain[...].astype(F32).reshape(1, width)
    loads[0].wait()
    x = nt(eye, tok_t[...])
    tok[...] = x.astype(BF16)
    first_scale = lax.rsqrt(jnp.mean(x * x, axis=-1, keepdims=True) + EPS)
    normed = (x * first_scale * gain1).astype(BF16)
    rows[dp] = widen(normed, lanes)
    loads[1].wait()
    for load in picks:
        load.start()
    k_all[blk] = nn(normed, wk[...]).astype(BF16)
    pl.semaphore_wait(barrier, len(partners))
    k_ring.start()
    loads[2].wait()
    v_all[blk] = nn(normed, wv[...]).astype(BF16)
    v_ring.start()

    y_other, core_other = 1 - row_y, 1 - core

    def row_push(k, slot, to, src=None):
        src = rows.at[slot] if src is None else src
        return push(src, rows.at[slot], row_send.at[k], row_recv.at[k], blk, to)

    other_dp = row_y * 2 + core_other

    def row_across():
        return row_push(0, dp, other_dp)

    def row_down():
        return row_push(1, dp, core)

    def row_on():
        return row_push(2, 2 + core, core_other)

    def row_up(src=None):
        return row_push(3 + core, dp, 2, src)

    def row_across_last():
        return row_push(7, dp, last_dp, brow)

    def row_last(src):
        return row_push(5 + core, dp, last_dp, src)

    lower = row_y == 0
    last = dp == last_dp

    def to_dp(o, who):
        return (dp + o) % n_dp == who

    pl.when(dp != 2)(lambda: row_across().start())
    pl.when(jnp.logical_not(lower))(lambda: row_down().start())

    loads[3].wait()
    q_all[blk] = nn(normed, wq[...]).astype(BF16)
    loads[4].wait()
    gat[1, own] = widen(nt(eye, cot_t[...]).astype(BF16), lanes)


    def gat_push(which, k, slot, to_blk, to_dp, at=slice(None)):
        ref = gat.at[which, slot, at]
        return push(ref, ref, gat_send.at[which, k], gat_recv.at[which, k], to_blk, to_dp)

    parts = [pl.ds(0, local // 2), pl.ds(local // 2, local // 2)]

    def gat_z(which, part):
        to = (z_other * n_near + z_near) * n_lo + lo
        return gat_push(which, part, own, to, dp, parts[part])

    def gat_y(which):
        return gat_push(which, 2, own, blk, y_other * 2 + core)

    def gat_y_far(which, part):
        slot = z_other * 4 + dp
        return gat_push(which, 3 + part, slot, blk, y_other * 2 + core, parts[part])

    def gat_core(which, a, b):
        slot = (z_far + a) % 2 * 4 + (row_y + b) % 2 * 2 + core
        return gat_push(which, 5 + a * 2 + b, slot, blk, row_y * 2 + core_other)

    def gat_far(which):
        for part in range(2):
            gat_z(which, part).start()

    def gat_start(which):
        gat_y(which).start()
        gat_core(which, 0, 0).start()

    def gat_forward(which, part):
        gat_z(which, part).wait_recv()
        gat_y_far(which, part).start()
        if part:
            gat_core(which, 1, 0).start()

    def gat_across(which, a):
        if a:
            for part in range(2):
                gat_y_far(which, part).wait_recv()
        else:
            gat_y(which).wait_recv()
        gat_core(which, a, 1).start()

    gat_start(1)
    r = lax.broadcasted_iota(jnp.int32, (cut, wide), 0)
    c = lax.broadcasted_iota(jnp.int32, (cut, wide), 1)
    for load in picks:
        load.wait()
    def pick_piece(k, carry):
        q, i = k // 3, k % 3
        column, start = piece_begin(q)
        pick = jnp.where(c - r == column - start, 1.0, 0.0).astype(BF16)
        piece = nt(pick, streams[i, q]).astype(BF16)
        held_w[i, pl.ds(pl.multiple_of(q * cut, 16), cut), :] = widen(piece, lanes)
        return carry

    lax.fori_loop(0, 3 * n_lo * n_near, pick_piece, 0)

    def stream(i, c):
        begin = pl.multiple_of(core * half_ff + c * chunk, chunk)
        slot = c % slots
        return pltpu.make_async_copy(
            feeds[i].at[:, pl.ds(begin, chunk)], streams.at[i, slot], stream_sem.at[i, slot]
        )

    def stream_next(i, c):
        pl.when(c + slots < n_chunk)(lambda: stream(i, c + slots).start())

    for c in range(slots):
        for i in (2, 0, 1):
            stream(i, c).start()
    k_ring.step_near()
    v_ring.step_near()

    near_span = 4 * local
    lane_near = lax.broadcasted_iota(jnp.int32, (8, near_span), 1)
    n_table = bucket_table.shape[0]
    n_bucket = bias_table.shape[1]
    held_lanes = 3 * LANES
    bucket = jnp.concatenate(
        [
            bucket_table[...].astype(F32).reshape(1, n_table),
            jnp.zeros((1, held_lanes - n_table), F32),
        ],
        axis=1,
    )
    bucket = jnp.broadcast_to(bucket, (8, held_lanes))
    turn = (
        lax.broadcasted_iota(jnp.int32, (held_lanes, held_lanes), 0)
        + lax.broadcasted_iota(jnp.int32, (held_lanes, held_lanes), 1)
        == n_table - 1
    ).astype(BF16)

    def bias_rows(line):
        line = jnp.concatenate([line, jnp.zeros((8, near_span - held_lanes), F32)], axis=1)
        line = jnp.where(lane_near >= n_table, line[:, n_table - 1 : n_table], line)
        moved = pltpu.roll(line, local - 1, 1)
        moved = jnp.where(lane_near < local - 1, line[:, 0:1], moved)
        hot = (
            jnp.broadcast_to(moved[0:1], (n_bucket, near_span))
            == lax.broadcasted_iota(jnp.int32, (n_bucket, near_span), 0).astype(F32)
        ).astype(F32)
        return hot, nn(bias_table[...], hot.astype(BF16))

    hots, tables[0] = bias_rows(bucket)
    onehot[...] = hots
    tables[1] = bias_rows(nn(bucket.astype(BF16), turn))[1]
    here_pos = blk * local + lax.broadcasted_iota(jnp.int32, (local, 1), 0)
    pack_pos = lax.broadcasted_iota(jnp.int32, (1, keys), 1)
    here_item = jnp.zeros((local, 1), jnp.int32)
    pack_item = jnp.zeros((1, keys), jnp.int32)
    end = jnp.int32(0)
    for m in range(lengths.shape[1]):
        end = end + lengths[0, m]
        here_item += (here_pos >= end).astype(jnp.int32)
        pack_item += (pack_pos >= end).astype(jnp.int32)

    near_at = pl.multiple_of(blk * local, local)
    inside = slice(local, local + keys)
    lane_lay = lax.broadcasted_iota(jnp.int32, (1, lay.shape[1]), 1)

    def bias_tile(turned, h):
        line = tables[turned, pl.ds(h, 1), :]
        ends_row = jnp.where(lane_lay < near_at, line[:, 0:1], line[:, near_span - 1 : near_span])
        lay[...] = jnp.broadcast_to(ends_row, lay.shape)
        rolled = pltpu.roll(
            jnp.broadcast_to(line, (local, near_span)), 1, 1, stride=1, stride_axis=0
        )
        lay[:, pl.ds(near_at, 3 * local)] = rolled[:, local:]
        return jnp.where(here_item == pack_item, lay[:, inside], -1e30)

    def fill_bias(h, carry):
        probs[h] = bias_tile(0, h)
        return carry

    lax.fori_loop(0, heads, fill_bias, 0)

    k_ring.step_far()
    gat_far(1)

    both = pl.ds((z_far * n_near + row_y) * 2, 2)
    gat_core(1, 0, 0).wait_recv()

    def hidden_slopes(c, carry):
        stream(2, c).wait()
        rows_c = gat[1, both].reshape(2 * local, lanes)[:, 0:width]
        slopes[c] = nn(rows_c, streams[2, c % slots]).astype(BF16)
        stream_next(2, c)
        return carry

    third = n_chunk // 3
    lax.fori_loop(0, third, hidden_slopes, 0)
    k_ring.step_last()
    v_ring.step_far()
    lax.fori_loop(third, n_chunk, hidden_slopes, 0)
    for c in range(slots):
        stream(2, c).start()
    k_ring.finish()

    @pl.when(lower)
    def _():
        row_down().wait_recv()
        row_on().start()

    lane = lax.broadcasted_iota(jnp.int32, (local, LANES), 1)
    low_half = lane < LANES // 2

    def halves(block):
        zero = jnp.zeros_like(block)
        return jnp.concatenate(
            [jnp.where(low_half, block, zero), jnp.where(low_half, zero, block)], axis=0
        )

    def joined(both):
        return jnp.where(low_half, both[0:local], both[local:])

    def pair_at(p):
        return pl.ds(pl.multiple_of(p * LANES, LANES), LANES)

    def cols_of(ref, p):
        return ref[:, :, pair_at(p)].reshape(keys, LANES)

    def softmax(p, stat):
        raw = nt(halves(q_all[blk, :, pair_at(p)]), cols_of(k_all, p))
        for s in range(2):
            h = 2 * p + s
            score = raw[s * local : (s + 1) * local] + probs[h]
            high = jnp.max(score, axis=-1, keepdims=True)
            expo = jnp.exp(score - high)
            total = jnp.sum(expo, axis=-1, keepdims=True)
            probs[h] = expo * (1.0 / total)
            stat = jnp.where(lane == h, high + jnp.log(total), stat)
        pl.when(p == 0)(v_ring.step_last)
        return stat

    stat = lax.fori_loop(0, pairs, softmax, jnp.zeros((local, LANES), F32))
    mine_at = pl.ds(pl.multiple_of(blk * local, local), local)

    def line_push(buf, send, recv, o):
        mine = buf.at[:, mine_at]
        return push(mine, mine, send.at[o], recv.at[o], (blk + o) % n_blk, dp)

    def total_push(o):
        return line_push(totals, lt_send, lt_recv, o)

    def delta_push(o):
        return line_push(deltas, de_send, de_recv, o)

    q_ring.start()
    totals[:, mine_at] = stat.T[0:8]
    for o in range(1, n_blk):
        total_push(o).start()
    v_ring.finish()

    def attend(p, carry):
        low = probs[pl.ds(2 * p, 2)].reshape(2 * local, keys).astype(BF16)
        attended[:, pair_at(p)] = joined(nn(low, cols_of(v_all, p)))
        return carry

    lax.fori_loop(0, pairs, attend, 0)

    gat_forward(1, 0)
    gat_forward(1, 1)
    gat_across(1, 0)
    loads[5].wait()
    attention = attended[...].astype(BF16)
    mid = tok[...].astype(F32) + nt(attention, wo[...])
    middle[...] = mid
    second_scale = lax.rsqrt(jnp.mean(mid * mid, axis=-1, keepdims=True) + EPS)
    gat[0, own] = widen((mid * second_scale * gain2).astype(BF16), lanes)
    gat_far(0)
    gat_start(0)

    grads_t[3] = attended[...].T.astype(BF16)

    mixed_acc[...] = jnp.zeros_like(mixed_acc)
    second_acc[...] = jnp.zeros_like(second_acc)
    gat_core(0, 0, 0).wait_recv()

    def feed(c, carry):
        slot = c % slots
        for i in range(3):
            stream(i, c).wait()
        normed2 = gat[0, both].reshape(2 * local, lanes)[:, 0:width]
        gate = nn(normed2, streams[0, slot])
        up = nn(normed2, streams[1, slot])
        hidden, gate_slope, up_slope = activation(gate, up, slopes[c].astype(F32))
        mixed_acc[...] += nt(hidden, streams[2, slot]).reshape(mixed_acc.shape)
        total = nt(gate_slope, streams[0, slot]) + nt(up_slope, streams[1, slot])
        second_acc[...] += total.reshape(second_acc.shape)
        for i in range(3):
            stream_next(i, c)
        return carry

    half = n_chunk // 2
    lax.fori_loop(0, half, feed, 0)
    q_ring.step_near()
    q_ring.step_far()
    gat_across(1, 1)
    lax.fori_loop(half, n_chunk - 1, feed, 0)
    gat_across(0, 0)
    q_ring.step_last()
    lax.fori_loop(n_chunk - 1, n_chunk, feed, 0)

    def swap_push():
        return push(swap_out, swap_in, swap_sem.at[0], swap_sem.at[1], blk, row_y * 2 + core_other)

    swap_out[0] = widen(second_acc[core_other].astype(BF16), lanes)
    swap_out[1] = widen(mixed_acc[core_other].astype(BF16), lanes)
    swap_push().start()
    gat_forward(0, 0)
    swap_push().wait_recv()

    mid = middle[...]
    second_scale = lax.rsqrt(jnp.mean(mid * mid, axis=-1, keepdims=True) + EPS)
    second_slope = second_acc[core] + swap_in[0, :, 0:width].astype(F32)
    small[...] = jnp.zeros_like(small)
    quarter = lanes // 4

    def small_line(first_row, line):
        line = widen(line, lanes)
        for q in range(4):
            at = slice(q * quarter, (q + 1) * quarter)
            small[first_row + q : first_row + q + 1, 0:quarter] = line[:, at]

    small_line(4, jnp.sum(second_slope * mid * second_scale, axis=0, keepdims=True))
    scaled = second_slope * gain2
    middle_slope = (
        gat[1, own, :, 0:width].astype(F32)
        + second_scale * scaled
        - mid
        * (second_scale * second_scale * second_scale)
        * jnp.mean(scaled * mid, axis=-1, keepdims=True)
    )
    mixed_acc[core] = mid + mixed_acc[core] + swap_in[1, :, 0:width].astype(F32)
    middle[...] = middle_slope
    branch = middle_slope.astype(BF16)
    s_all[blk] = nn(branch, wo[...]).astype(BF16)
    s_ring.start()
    product = s_all[blk].astype(F32) * attended[...]
    delta_cols = jnp.zeros((local, LANES), F32)
    for h in range(heads):
        piece = product[:, (h // 2) * LANES : (h // 2 + 1) * LANES]
        mine = low_half if h % 2 == 0 else jnp.logical_not(low_half)
        delta = jnp.sum(jnp.where(mine, piece, 0.0), axis=-1, keepdims=True)
        delta_cols = jnp.where(lane == h, delta, delta_cols)
    deltas[:, mine_at] = delta_cols.T[0:8]
    for o in range(1, n_blk):
        delta_push(o).start()

    swap_push().wait_send()
    brow = swap_out.at[0]
    brow[...] = widen(branch, lanes)

    @pl.when(last)
    def _():
        row_across().wait_send()
        row_down().wait_send()
        rows[dp] = widen(branch, lanes)

    def col_push(o):
        to = (dp + o) % n_dp
        begin = pl.multiple_of(dp * local, local)
        return push(
            grads_t.at[to],
            acol.at[:, pl.ds(begin, local)],
            col_send.at[o],
            col_recv.at[o],
            blk,
            to,
        )


    step = 2 * local
    held = held_w.shape[1]

    def recompute(k, carry):
        a, b = k // 2, k % 2

        @pl.when(k > 0)
        def _():
            for which in range(2):
                gat_core(which, a, b).wait_recv()

        t = (z_far + a) % 2 * n_near + (row_y + b) % 2
        rows_n = gat[0, pl.ds(2 * t, 2)].reshape(step, lanes)
        rows_c = gat[1, pl.ds(2 * t, 2)].reshape(step, lanes)
        gate = nt(held_w[0], rows_n)
        up = nt(held_w[1], rows_n)
        hidden_slope = nt(held_w[2], rows_c)
        hidden, gate_slope, up_slope = activation(gate, up, hidden_slope)
        streams[0, t, 0:held, :] = gate_slope
        streams[1, t, 0:held, :] = up_slope
        streams[2, t, 0:held, :] = hidden
        return carry

    lax.fori_loop(0, 1, recompute, 0)
    gat_forward(0, 1)
    s_ring.step_near()
    pl.when(lower)(lambda: row_last(brow).start())
    pl.when(dp == 2)(lambda: row_across_last().start())

    flip = (
        lax.broadcasted_iota(jnp.int32, (local, local), 0)
        + lax.broadcasted_iota(jnp.int32, (local, local), 1)
        == local - 1
    ).astype(BF16)
    diag[...] = jnp.zeros_like(diag)
    lay[...] = jnp.zeros_like(lay)
    def query_side(p, carry):
        dots = nt(halves(s_all[blk, :, pair_at(p)]), cols_of(v_all, p))
        ds = []
        for s in range(2):
            h = 2 * p + s
            delta = jnp.sum(jnp.where(lane == h, delta_cols, 0.0), axis=-1, keepdims=True)
            one = (probs[h] * (dots[s * local : (s + 1) * local] - delta)).astype(BF16)
            wide_one = one.astype(F32)
            lay[:, inside] = wide_one
            near = lay[:, pl.ds(near_at, 3 * local)].astype(BF16)
            padded = jnp.concatenate([nn(flip, near), jnp.zeros((local, local), F32)], axis=1)
            skewed = pltpu.roll(padded, 0, 1, stride=1, stride_axis=0)
            total = jnp.sum(wide_one, axis=0, keepdims=True)
            before = jnp.sum(jnp.where(pack_pos < near_at - local, total, 0.0), axis=1, keepdims=True)
            after = jnp.sum(
                jnp.where(pack_pos >= near_at + 2 * local, total, 0.0), axis=1, keepdims=True
            )
            line = jnp.sum(skewed, axis=0, keepdims=True)
            line = line + jnp.where(lane_near[0:1] == 0, before, 0.0)
            diag[pl.ds(h, 1), :] = line + jnp.where(lane_near[0:1] == near_span - 1, after, 0.0)
            ds.append(one)
        dq = joined(nn(jnp.concatenate(ds, axis=0), cols_of(k_all, p)))
        dq_rows[:, pair_at(p)] = dq.astype(BF16)
        grads_t[0, pair_at(p), :] = dq.T.astype(BF16)
        return carry

    lax.fori_loop(0, pairs, query_side, 0)
    for o in range(1, n_dp):
        pl.when(jnp.logical_or(to_dp(o, 0), to_dp(o, last_dp)))(lambda o=o: col_push(o).start())
    pl.when(lower)(lambda: row_up().start())
    s_ring.step_far()
    lax.fori_loop(1, 2, recompute, 0)

    q_ring.finish()
    for o in range(1, n_blk):
        total_push(o).wait_recv()

    def key_weights(p, carry):
        raw = nt(halves(k_all[blk, :, pair_at(p)]), cols_of(q_all, p))
        for s in range(2):
            h = 2 * p + s
            piece = slice(s * local, (s + 1) * local)
            probs[h] = jnp.exp(raw[piece] + bias_tile(1, h) - totals[pl.ds(h, 1), :])
        return carry

    lax.fori_loop(0, pairs, key_weights, 0)

    gat_across(0, 1)
    s_ring.step_last()
    lax.fori_loop(2, HI, recompute, 0)

    lo_far, near_far = 1 - lo, 1 - z_near
    along_lo_blk = hi * n_lo + lo_far
    along_z_blk = (z_far * n_near + near_far) * n_lo + lo

    def split():
        return slice(0, 48), slice(48, cut)

    def ff_hop(src, dst, w, k, to_blk):
        return push(src, dst, ff_send.at[w, k], ff_sem.at[w, k], to_blk, dp)

    def ff_hop1(w):
        by_lo, by_z = split()
        return (
            ff_hop(ff_part.at[w, lo_far, :, by_lo], ff_r1.at[w, :, by_lo], w, 0, along_lo_blk),
            ff_hop(ff_part.at[w, :, near_far, by_z], ff_r1.at[w, :, by_z], w, 1, along_z_blk),
        )

    def ff_hop2(w):
        by_lo, by_z = split()
        return (
            ff_hop(ff_part.at[w, lo, near_far, by_lo], ff_r2.at[w, by_lo], w, 2, along_z_blk),
            ff_hop(ff_part.at[w, lo_far, z_near, by_z], ff_r2.at[w, by_z], w, 3, along_lo_blk),
        )

    def ff_middle(w):
        by_lo, by_z = split()
        one, two = ff_hop1(w)
        far, near = ff_hop2(w)
        one.wait_recv()
        ff_part[w, lo, near_far, by_lo] = (
            ff_part[w, lo, near_far, by_lo].astype(F32) + ff_r1[w, near_far, by_lo].astype(F32)
        ).astype(BF16)
        far.start()
        two.wait_recv()
        ff_part[w, lo_far, z_near, by_z] = (
            ff_part[w, lo_far, z_near, by_z].astype(F32) + ff_r1[w, lo_far, by_z].astype(F32)
        ).astype(BF16)
        near.start()

    def ff_last(w):
        by_lo, by_z = split()
        far, near = ff_hop2(w)
        far.wait_recv()
        near.wait_recv()
        mine = ff_part[w, lo, z_near].astype(F32) + ff_r2[w].astype(F32)
        ff_out[w, by_lo] = mine[by_lo] + ff_r1[w, z_near, by_lo].astype(F32)
        ff_out[w, by_z] = mine[by_z] + ff_r1[w, lo, by_z].astype(F32)

    def at_hop1():
        to = hi * n_lo + 1 - lo
        return push(at_part.at[1 - lo], at_first, at_send.at[0], at_sem.at[0], to, dp)

    def at_hop2(o):
        to = (hi + o) % HI
        return push(
            at_part.at[lo, to], at_recv.at[hi], at_send.at[o], at_sem.at[o], to * n_lo + lo, dp
        )

    def attention_gradient():
        acol[:, pl.ds(pl.multiple_of(dp * local, local), local)] = grads_t[dp]

        @pl.when(lower)
        def _():
            row_across().wait_recv()
            row_on().wait_recv()

        @pl.when(dp == 2)
        def _():
            row_across().wait_recv()
            for k in (3, 4):
                row_push(k, dp, 2).wait_recv()

        @pl.when(last)
        def _():
            for k in (5, 6, 7):
                row_push(k, dp, last_dp).wait_recv()

        for o in range(1, n_dp):
            col_push(o).wait_recv()
        total = nn(acol[...], rows[...].reshape(n_dp * local, lanes))
        total = total.astype(BF16).reshape(n_blk, inner // n_blk, lanes)
        for b in range(n_blk):
            at_part[b % n_lo, b // n_lo] = total[b]
        at_hop1().start()

    def attention_gradient_next():
        at_hop1().wait_recv()
        at_part[lo] = (at_part[lo].astype(F32) + at_first[...].astype(F32)).astype(BF16)
        for o in range(1, HI):
            at_hop2(o).start()
        at_recv[hi] = at_part[lo, hi]

    early = jnp.logical_or(dp == 0, dp == last_dp)

    order = (2, 0, 1)

    def gradient(k, carry):
        w = (k + 2) % 3
        left = jnp.concatenate([streams[w, t, 0:held, :] for t in range(HI)], axis=1)
        total = nn(left, gat[w // 2].reshape(2 * HI * local, lanes))
        ff_part[w] = total.astype(BF16).reshape(n_lo, n_near, cut, lanes)
        for hop in ff_hop1(w):
            hop.start()
        return carry

    pl.when(early)(attention_gradient)
    lax.fori_loop(0, 1, gradient, 0)

    s_ring.finish()
    for o in range(1, n_blk):
        delta_push(o).wait_recv()

    def key_side(p, carry):
        queries = cols_of(q_all, p)
        slopes_p = cols_of(s_all, p)
        dots = nt(halves(v_all[blk, :, pair_at(p)]), slopes_p)
        low = []
        ds = []
        for s in range(2):
            h = 2 * p + s
            prob = probs[h]
            low.append(prob.astype(BF16))
            dot = dots[s * local : (s + 1) * local]
            ds.append((prob * (dot - deltas[pl.ds(h, 1), :])).astype(BF16))
        dk = joined(nn(jnp.concatenate(ds, axis=0), queries))
        dv = joined(nn(jnp.concatenate(low, axis=0), slopes_p))
        grads_t[1, pair_at(p), :] = dk.T.astype(BF16)
        grads_t[2, pair_at(p), :] = dv.T.astype(BF16)
        return carry

    lax.fori_loop(0, pairs, key_side, 0)
    for o in range(1, n_dp):
        middle_two = jnp.logical_or(to_dp(o, 1), to_dp(o, 2))
        pl.when(middle_two)(lambda o=o: col_push(o).start())

    lax.fori_loop(1, 2, gradient, 0)
    ff_middle(order[0])
    bias_grad = lax.dot_general(
        diag[...],
        onehot[...],
        (((1,), (1,)), ((), ())),
        precision=lax.Precision.HIGHEST,
        preferred_element_type=F32,
    )
    small[0:heads, quarter : quarter + n_bucket] = bias_grad[0:heads]

    pl.when(jnp.logical_not(early))(attention_gradient)
    lax.fori_loop(2, 3, gradient, 0)

    x = tok[...].astype(F32)
    first_scale = lax.rsqrt(jnp.mean(x * x, axis=-1, keepdims=True) + EPS)
    key_slope = grads_t[1].astype(F32).T.astype(BF16)
    value_slope = grads_t[2].astype(F32).T.astype(BF16)
    first_slope = nt(dq_rows[...], wq[...]) + nt(key_slope, wk[...]) + nt(value_slope, wv[...])
    small_line(0, jnp.sum(first_slope * x * first_scale, axis=0, keepdims=True))

    def small_blk_push(o):
        return push(small, small_blk.at[blk], sb_send.at[o], sb_sem.at[o], (blk + o) % n_blk, dp)

    for o in range(1, n_blk):
        small_blk_push(o).start()
    small_blk[blk] = small[...]
    scaled = first_slope * gain1
    token_slope = (
        middle[...]
        + first_scale * scaled
        - x
        * (first_scale * first_scale * first_scale)
        * jnp.mean(scaled * x, axis=-1, keepdims=True)
    )
    tokgrad_out[...] = token_slope.T

    ff_middle(order[1])
    attention_gradient_next()
    for o in range(1, n_blk):
        small_blk_push(o).wait_recv()
    total = small_blk[0]
    for b in range(1, n_blk):
        total += small_blk[b]
    small_dp[dp] = total

    def small_dp_push(o):
        return push(
            small_dp.at[dp], small_dp.at[dp], sd_send.at[o], sd_sem.at[o], blk, (dp + o) % n_dp
        )

    for o in range(1, n_dp):
        small_dp_push(o).start()

    ff_middle(order[2])
    mixed_out[...] = mixed_acc[core].T.astype(BF16)
    for o in range(1, HI):
        at_hop2(o).wait_recv()
    total = at_recv[0].astype(F32)
    for b in range(1, HI):
        total += at_recv[b].astype(F32)
    ag[dp] = total.astype(BF16)

    def ag_push(o):
        return push(ag.at[dp], ag.at[dp], ag_send.at[o], ag_sem.at[o], blk, (dp + o) % n_dp)

    for o in range(1, n_dp):
        ag_push(o).start()
    for w in order:
        ff_last(w)

    for o in range(1, n_dp):
        small_dp_push(o).wait_recv()
        ag_push(o).wait_recv()
    total = small_dp[0]
    for d in range(1, n_dp):
        total += small_dp[d]
    small_out[...] = jnp.zeros_like(small_out)
    for q in range(4):
        at = slice(q * quarter, (q + 1) * quarter)
        small_out[0:1, at] = total[q : q + 1, 0:quarter]
        small_out[1:2, at] = total[4 + q : 5 + q, 0:quarter]
    small_out[2 : 2 + heads, 0:n_bucket] = total[0:heads, quarter : quarter + n_bucket]
    for a in range(4):
        attn_out[a] = ag[a].astype(F32)

    for ring in (k_ring, v_ring, q_ring, s_ring):
        ring.drain()
    for which in range(2):
        gat_y(which).wait_send()
        for a in range(2):
            gat_z(which, a).wait_send()
            gat_y_far(which, a).wait_send()
            for b in range(2):
                gat_core(which, a, b).wait_send()

    @pl.when(lower)
    def _():
        row_across().wait_send()
        row_on().wait_send()
        row_up().wait_send()
        row_last(brow).wait_send()

    @pl.when(dp == 2)
    def _():
        row_down().wait_send()
        row_across_last().wait_send()

    for o in range(1, n_dp):
        col_push(o).wait_send()
        small_dp_push(o).wait_send()
        ag_push(o).wait_send()
    for o in range(1, n_blk):
        total_push(o).wait_send()
        delta_push(o).wait_send()
        small_blk_push(o).wait_send()
    at_hop1().wait_send()
    for o in range(1, HI):
        at_hop2(o).wait_send()
    for w in order:
        for hop in ff_hop1(w) + ff_hop2(w):
            hop.wait_send()


def spread_kernel(small, mixed, tokens_gradient, attn, ff_grads, *outs):
    gain1, gain2, bias, mixed_out, tokens_out = outs[:5]
    width = gain1.shape[0]
    gain1[...] = small[0, 0:width]
    gain2[...] = small[1, 0:width]
    bias[...] = small[2 : 2 + bias.shape[0], 0 : bias.shape[1]]
    mixed_out[...] = mixed[...]
    tokens_out[...] = tokens_gradient[...]
    for a in range(4):
        outs[5 + a][...] = attn[a, :, 0:width]
    for w in range(3):
        outs[9 + w][...] = ff_grads[w, :, 0:width]


def fused(
    n_blk,
    n_dp,
    tokens,
    lengths,
    bucket_table,
    first_gain,
    position_bias,
    w_query,
    w_key,
    w_value,
    w_output,
    second_gain,
    w_gate,
    w_up,
    w_down,
    cotangent,
):
    local, width = tokens.shape[1:]
    inner = w_query.shape[1]
    ff = w_gate.shape[1]
    n_bucket, heads = position_bias.shape
    keys = n_blk * local
    cut = ff // (n_blk * n_dp)
    n_lo = n_blk // HI
    held = n_lo * (HI // 2) * cut
    part = inner // n_blk
    pairs = inner // LANES
    chunk = 256
    lanes = -(-width // LANES) * LANES
    dma, vmem = pltpu.SemaphoreType.DMA, pltpu.VMEM
    any_spec = pl.BlockSpec(memory_space=pl.ANY)
    vmem_spec = pl.BlockSpec(memory_space=pltpu.VMEM)
    smem_spec = pl.BlockSpec(memory_space=pltpu.SMEM)
    scratch = [
        vmem((width, local), BF16),
        vmem((width, local), BF16),
        vmem((local, width), BF16),
        vmem((width, inner), BF16),
        vmem((width, inner), BF16),
        vmem((width, inner), BF16),
        vmem((width, inner), BF16),
        vmem((n_blk, local, inner), BF16),
        vmem((n_blk, local, inner), BF16),
        vmem((n_blk, local, inner), BF16),
        vmem((n_blk, local, inner), BF16),
        vmem((8, keys), F32),
        vmem((8, keys), F32),
        vmem((2 * pairs, local, keys), F32),
        vmem((local, inner), BF16),
        vmem((2, 2 * HI, local, lanes), BF16),
        vmem((3, 4, width, chunk), BF16),
        vmem((3, held, lanes), BF16),
        vmem((ff // 2 // chunk, 2 * local, chunk), BF16),
        vmem((local, width), F32),
        vmem((2, local, width), F32),
        vmem((2, local, width), F32),
        vmem((local, inner), F32),
        vmem((2, local, lanes), BF16),
        vmem((2, local, lanes), BF16),
        vmem((3, n_lo, HI // 2, cut, lanes), BF16),
        vmem((3, 2, cut, lanes), BF16),
        vmem((3, cut, lanes), BF16),
        vmem((n_dp, local, lanes), BF16),
        vmem((inner, n_dp * local), BF16),
        vmem((4, inner, local), BF16),
        vmem((n_lo, HI, part, lanes), BF16),
        vmem((HI, part, lanes), BF16),
        vmem((HI, part, lanes), BF16),
        vmem((n_dp, part, lanes), BF16),
        vmem((8, lanes // 4 + LANES), F32),
        vmem((n_blk, 8, lanes // 4 + LANES), F32),
        vmem((n_dp, 8, lanes // 4 + LANES), F32),
        vmem((2, heads + heads % 2, 4 * local), F32),
        vmem((n_bucket, 4 * local), F32),
        vmem((8, 4 * local), F32),
        vmem((local, keys + 2 * local), F32),
        dma((6,)),
        dma((3, 4)),
        dma((2,)),
    ]
    for shape in (
        (7,),
        (7,),
        (7,),
        (7,),
        (n_blk,),
        (n_blk,),
        (2, 9),
        (8,),
        (n_dp,),
        (3, 4),
        (HI,),
        (n_dp,),
        (n_blk,),
        (n_dp,),
    ):
        scratch += [dma(shape), dma(shape)]
    mixed, tokens_gradient, small, attn, ff_grads = pl.pallas_call(
        functools.partial(layer_kernel, n_blk, n_dp),
        out_shape=(
            jax.ShapeDtypeStruct((width, local), BF16),
            jax.ShapeDtypeStruct((width, local), F32),
            jax.ShapeDtypeStruct((8, lanes), F32),
            jax.ShapeDtypeStruct((4, part, lanes), F32),
            jax.ShapeDtypeStruct((3, cut, lanes), F32),
        ),
        in_specs=[smem_spec] + [vmem_spec] * 4 + [any_spec] * 9,
        out_specs=(vmem_spec,) * 5,
        scratch_shapes=scratch,
        compiler_params=pltpu.CompilerParams(
            collective_id=0, has_side_effects=True, vmem_limit_bytes=64 * 1024 * 1024 - 65536
        ),
    )(
        lengths,
        bucket_table,
        first_gain,
        second_gain,
        position_bias.T,
        tokens[0].T,
        cotangent[0].T,
        w_query,
        w_key,
        w_value,
        w_output.T,
        w_gate,
        w_up,
        w_down.T,
    )
    outs = pl.pallas_call(
        spread_kernel,
        out_shape=[
            jax.ShapeDtypeStruct((width,), F32),
            jax.ShapeDtypeStruct((width,), F32),
            jax.ShapeDtypeStruct((heads, n_bucket), F32),
            jax.ShapeDtypeStruct((width, local), BF16),
            jax.ShapeDtypeStruct((width, local), F32),
        ]
        + [jax.ShapeDtypeStruct((part, width), F32)] * 4
        + [jax.ShapeDtypeStruct((cut, width), F32)] * 3,
        in_specs=[vmem_spec] * 5,
        out_specs=[vmem_spec] * 12,
    )(small, mixed, tokens_gradient, attn, ff_grads)
    gain1, gain2, bias, mixed, tokens_gradient, query, key, value, output, gate, up, down = outs
    return (
        mixed.T[None],
        tokens_gradient.T[None],
        gain1,
        bias.T,
        query.T,
        key.T,
        value.T,
        output,
        gain2,
        gate.T,
        up.T,
        down,
    )


def normalize(values, gain):
    return values * lax.rsqrt(jnp.mean(values * values, axis=-1, keepdims=True) + 1e-06) * gain


def gelu_tanh(values):
    return (
        0.5
        * values
        * (
            1.0
            + jnp.tanh(math.sqrt(2.0 / math.pi) * (values + 0.044715 * values * values * values))
        )
    )


def activate(gate, up_part):
    return gelu_tanh(gate) * up_part


def blocked(block_fn, carry, piece):
    count = piece[0].shape[0]
    size = 512
    parts = tuple((arr.reshape((count // size, size) + arr.shape[1:]) for arr in piece))

    def visit(state, inputs):
        number, block = inputs
        return (block_fn(state, block, number * size), None)

    state, _ = lax.scan(visit, carry, (jnp.arange(count // size, dtype=jnp.int32), parts))
    return state


def diagonal_sums(slope, shift, reach, table_len):
    heads, rows, cols = slope.shape
    width = rows + cols
    flipped = slope[:, ::-1, :]
    padded = jnp.pad(flipped, ((0, 0), (0, 0), (0, rows)))
    skewed = padded.reshape(heads, rows * width)[:, : rows * (width - 1)].reshape(
        heads, rows, width - 1
    )
    diagonal = jnp.sum(skewed, axis=1)
    relative = shift + jnp.arange(width - 1, dtype=jnp.int32) - (rows - 1)
    index = jnp.clip(relative, -reach, reach) + reach
    selector = (index[:, None] == jnp.arange(table_len, dtype=jnp.int32)[None, :]).astype(
        jnp.float32
    )
    return jnp.dot(
        diagonal, selector, precision=lax.Precision.HIGHEST, preferred_element_type=jnp.float32
    )


def on_device(
    tokens,
    lengths,
    bucket_table,
    first_gain,
    position_bias,
    w_query,
    w_key,
    w_value,
    w_output,
    second_gain,
    w_gate,
    w_up,
    w_down,
    cotangent,
):
    f32 = jnp.float32
    bf16 = jnp.bfloat16
    heads = position_bias.shape[1]
    inner = w_query.shape[1]
    head_size = inner // heads
    local = tokens.shape[1]
    table_len = bucket_table.shape[0]
    reach = (table_len - 1) // 2
    inputs = tokens[0].astype(f32)
    positions = lax.axis_index("blk") * local + jnp.arange(local, dtype=jnp.int32)
    ends = jnp.cumsum(lengths[0])
    onehot = (
        bucket_table[:, None] == jnp.arange(position_bias.shape[0], dtype=jnp.int32)[None, :]
    ).astype(f32)
    head_rows = jnp.einsum(
        "rb,bh->hr", onehot, position_bias.astype(f32), precision=lax.Precision.HIGHEST
    )

    def item_of(places):
        return jnp.sum((places[:, None] >= ends[None, :]).astype(jnp.int32), axis=1)

    def pair_scores(query3, key3, query_pos, key_pos):
        offset = jnp.clip(key_pos[None, :] - query_pos[:, None], -reach, reach) + reach
        raw = jnp.einsum("qhd,khd->hqk", query3, key3, preferred_element_type=f32) + jnp.take(
            head_rows, offset, axis=1
        )
        mask = item_of(query_pos)[:, None] == item_of(key_pos)[None, :]
        return (jnp.where(mask[None], raw, -1e30), mask)

    normed_first, first_back = jax.vjp(normalize, inputs, first_gain.astype(f32))
    normed_first_low = normed_first.astype(bf16)
    queries = jnp.dot(normed_first_low, w_query, preferred_element_type=f32).astype(bf16)
    keys_low = jnp.dot(normed_first_low, w_key, preferred_element_type=f32).astype(bf16)
    values_low = jnp.dot(normed_first_low, w_value, preferred_element_type=f32).astype(bf16)
    query3 = queries.reshape(local, heads, head_size)
    key3_own = keys_low.reshape(local, heads, head_size)
    value3_own = values_low.reshape(local, heads, head_size)

    def forward_block(state, piece, start):
        high, total, running = state
        key_piece, value_piece = piece
        count = key_piece.shape[0]
        key_pos = start + jnp.arange(count, dtype=jnp.int32)
        scores, mask = pair_scores(
            query3, key_piece.reshape(count, heads, head_size), positions, key_pos
        )
        new_high = jnp.maximum(high, jnp.max(scores, axis=-1))
        weights = jnp.where(mask[None], jnp.exp(scores - new_high[..., None]), 0.0)
        factor = jnp.exp(high - new_high)
        total = total * factor + jnp.sum(weights, axis=-1)
        running = running * factor.T[:, :, None] + jnp.einsum(
            "hqk,khd->qhd",
            weights.astype(bf16),
            value_piece.reshape(count, heads, head_size),
            preferred_element_type=f32,
        )
        return (new_high, total, running)

    start_state = (
        jnp.full((heads, local), -1e30, f32),
        jnp.zeros((heads, local), f32),
        jnp.zeros((local, heads, head_size), f32),
    )
    high, total, running = blocked(
        forward_block,
        start_state,
        (
            lax.all_gather(keys_low, "blk", axis=0, tiled=True),
            lax.all_gather(values_low, "blk", axis=0, tiled=True),
        ),
    )
    log_total = high + jnp.log(total)
    attended = running / total.T[:, :, None]
    attention = attended.reshape(local, inner).astype(bf16)
    middle = inputs + jnp.dot(attention, w_output, preferred_element_type=f32)
    normed_second, second_back = jax.vjp(normalize, middle, second_gain.astype(f32))
    normed_second_low = normed_second.astype(bf16)
    gate = jnp.dot(normed_second_low, w_gate, preferred_element_type=f32)
    up_part = jnp.dot(normed_second_low, w_up, preferred_element_type=f32)
    hidden, activate_back = jax.vjp(activate, gate, up_part)
    hidden_low = hidden.astype(bf16)
    mixed = (middle + jnp.dot(hidden_low, w_down, preferred_element_type=f32)).astype(bf16)
    upstream = cotangent[0]
    down_local = jnp.einsum("td,tf->df", upstream, hidden_low, preferred_element_type=f32)
    hidden_slope = jnp.einsum("td,fd->tf", upstream, w_down, preferred_element_type=f32)
    gate_raw, up_raw = activate_back(hidden_slope)
    gate_slope = gate_raw.astype(bf16)
    up_slope = up_raw.astype(bf16)
    gate_local = jnp.einsum("td,tf->df", normed_second_low, gate_slope, preferred_element_type=f32)
    up_local = jnp.einsum("td,tf->df", normed_second_low, up_slope, preferred_element_type=f32)
    second_slope = jnp.einsum(
        "tf,df->td", gate_slope, w_gate, preferred_element_type=f32
    ) + jnp.einsum("tf,df->td", up_slope, w_up, preferred_element_type=f32)
    middle_norm_slope, second_gain_local = second_back(second_slope)
    middle_slope = upstream.astype(f32) + middle_norm_slope
    feed_parts = None
    branch_slope = middle_slope.astype(bf16)
    output_local = jnp.einsum("td,ti->di", branch_slope, attention, preferred_element_type=f32)
    attention_slope = jnp.einsum(
        "td,id->ti", branch_slope, w_output, preferred_element_type=f32
    ).astype(bf16)
    slope3 = attention_slope.reshape(local, heads, head_size)
    delta_rows = jnp.sum(slope3.astype(f32) * attended, axis=-1)
    delta_heads = delta_rows.T

    def query_block(state, piece, start):
        query_acc, table_acc = state
        key_piece, value_piece = piece
        count = key_piece.shape[0]
        key_pos = start + jnp.arange(count, dtype=jnp.int32)
        key3 = key_piece.reshape(count, heads, head_size)
        scores, mask = pair_scores(query3, key3, positions, key_pos)
        weights = jnp.where(mask[None], jnp.exp(scores - log_total[..., None]), 0.0)
        value_dots = jnp.einsum(
            "qhd,khd->hqk",
            slope3,
            value_piece.reshape(count, heads, head_size),
            preferred_element_type=f32,
        )
        score_slope = (weights * (value_dots - delta_heads[..., None])).astype(bf16)
        query_acc = query_acc + jnp.einsum(
            "hqk,khd->qhd", score_slope, key3, preferred_element_type=f32
        )
        table_acc = table_acc + diagonal_sums(
            score_slope.astype(f32), start - positions[0], reach, table_len
        )
        return (query_acc, table_acc)

    query_init = (jnp.zeros((local, heads, head_size), f32), jnp.zeros((heads, table_len), f32))
    query_acc, table_acc = blocked(
        query_block,
        query_init,
        (
            lax.all_gather(keys_low, "blk", axis=0, tiled=True),
            lax.all_gather(values_low, "blk", axis=0, tiled=True),
        ),
    )
    whole_total, whole_delta = (
        lax.all_gather(log_total.T, "blk", axis=0, tiled=True),
        lax.all_gather(delta_rows, "blk", axis=0, tiled=True),
    )

    def key_block(state, piece, start):
        key_acc, value_acc = state
        query_piece, slope_piece = piece
        count = query_piece.shape[0]
        query_pos = start + jnp.arange(count, dtype=jnp.int32)
        query3p = query_piece.reshape(count, heads, head_size)
        slope3p = slope_piece.reshape(count, heads, head_size)
        scores, mask = pair_scores(query3p, key3_own, query_pos, positions)
        piece_total = lax.dynamic_slice_in_dim(whole_total, start, count, 0).T
        piece_delta = lax.dynamic_slice_in_dim(whole_delta, start, count, 0).T
        weights = jnp.where(mask[None], jnp.exp(scores - piece_total[..., None]), 0.0)
        value_dots = jnp.einsum("qhd,khd->hqk", slope3p, value3_own, preferred_element_type=f32)
        score_slope = (weights * (value_dots - piece_delta[..., None])).astype(bf16)
        key_acc = key_acc + jnp.einsum(
            "hqk,qhd->khd", score_slope, query3p, preferred_element_type=f32
        )
        value_acc = value_acc + jnp.einsum(
            "hqk,qhd->khd", weights.astype(bf16), slope3p, preferred_element_type=f32
        )
        return (key_acc, value_acc)

    key_init = (
        jnp.zeros((local, heads, head_size), f32),
        jnp.zeros((local, heads, head_size), f32),
    )
    key_acc, value_acc = blocked(
        key_block,
        key_init,
        (
            lax.all_gather(queries, "blk", axis=0, tiled=True),
            lax.all_gather(attention_slope, "blk", axis=0, tiled=True),
        ),
    )
    query_slope = query_acc.reshape(local, inner).astype(bf16)
    key_slope = key_acc.reshape(local, inner).astype(bf16)
    value_slope = value_acc.reshape(local, inner).astype(bf16)
    query_local = jnp.einsum("td,ti->di", normed_first_low, query_slope, preferred_element_type=f32)
    key_local = jnp.einsum("td,ti->di", normed_first_low, key_slope, preferred_element_type=f32)
    value_local = jnp.einsum("td,ti->di", normed_first_low, value_slope, preferred_element_type=f32)
    first_slope = (
        jnp.einsum("ti,di->td", query_slope, w_query, preferred_element_type=f32)
        + jnp.einsum("ti,di->td", key_slope, w_key, preferred_element_type=f32)
        + jnp.einsum("ti,di->td", value_slope, w_value, preferred_element_type=f32)
    )
    input_norm_slope, first_gain_local = first_back(first_slope)
    tokens_gradient = middle_slope + input_norm_slope
    bias_local = jnp.einsum("rb,hr->bh", onehot, table_acc, precision=lax.Precision.HIGHEST)
    feed_parts = (
        lax.psum_scatter(gate_local, ("blk", "dp"), scatter_dimension=1, tiled=True),
        lax.psum_scatter(up_local, ("blk", "dp"), scatter_dimension=1, tiled=True),
        lax.psum_scatter(down_local, ("blk", "dp"), scatter_dimension=1, tiled=True),
    )
    attention_parts = (
        lax.psum_scatter(
            query_local.astype(jnp.bfloat16), "blk", scatter_dimension=1, tiled=True
        ).astype(jnp.float32),
        lax.psum_scatter(
            key_local.astype(jnp.bfloat16), "blk", scatter_dimension=1, tiled=True
        ).astype(jnp.float32),
        lax.psum_scatter(
            value_local.astype(jnp.bfloat16), "blk", scatter_dimension=1, tiled=True
        ).astype(jnp.float32),
        lax.psum_scatter(
            output_local.astype(jnp.bfloat16), "blk", scatter_dimension=1, tiled=True
        ).astype(jnp.float32),
    )
    attention_parts = (
        lax.psum(attention_parts[0].astype(jnp.bfloat16), "dp").astype(jnp.float32),
        lax.psum(attention_parts[1].astype(jnp.bfloat16), "dp").astype(jnp.float32),
        lax.psum(attention_parts[2].astype(jnp.bfloat16), "dp").astype(jnp.float32),
        lax.psum(attention_parts[3].astype(jnp.bfloat16), "dp").astype(jnp.float32),
    )
    first_total, bias_total, second_total = lax.psum(
        (first_gain_local, bias_local, second_gain_local), ("blk", "dp")
    )
    return (
        mixed[None],
        tokens_gradient[None],
        first_total,
        bias_total,
        attention_parts[0],
        attention_parts[1],
        attention_parts[2],
        attention_parts[3].T,
        second_total,
        feed_parts[0],
        feed_parts[1],
        feed_parts[2].T,
    )


def solution(mesh):
    n_blk, n_dp = mesh.shape["blk"], mesh.shape["dp"]

    def on_any(*args):
        local = args[0].shape[1]
        inner, ff = args[5].shape[1], args[10].shape[1]
        fits = n_blk * local <= 1024 and n_dp == 4 and n_blk == 2 * HI
        if fits and ff % (16 * n_blk * n_dp) == 0 and inner % (16 * n_blk) == 0:
            return fused(n_blk, n_dp, *args)
        return on_device(*args)

    return jax.shard_map(
        on_any,
        mesh=mesh,
        in_specs=(
            P("dp", "blk", None),
            P("dp", None),
            P(),
            P(),
            P(),
            P(),
            P(),
            P(),
            P(),
            P(),
            P(),
            P(),
            P(),
            P("dp", "blk", None),
        ),
        out_specs=(
            P("dp", "blk", None),
            P("dp", "blk", None),
            P(),
            P(),
            P(None, "blk"),
            P(None, "blk"),
            P(None, "blk"),
            P("blk", None),
            P(),
            P(None, ("blk", "dp")),
            P(None, ("blk", "dp")),
            P(("blk", "dp"), None),
        ),
        check_vma=False,
    )
```

```python
import functools
import math

import jax
import jax.numpy as jnp
from jax import lax
from jax.experimental import pallas as pl
from jax.experimental.pallas import tpu as pltpu
from jax.sharding import PartitionSpec as P

F32 = jnp.float32
BF16 = jnp.bfloat16
EPS = 1e-06
ROOT = math.sqrt(2.0 / math.pi)
HI = 4
LANES = 128


def nn(left, right):
    return lax.dot_general(left, right, (((1,), (0,)), ((), ())), preferred_element_type=F32)


def nt(left, right):
    return lax.dot_general(left, right, (((1,), (1,)), ((), ())), preferred_element_type=F32)


def tn(left, right):
    return lax.dot_general(left, right, (((0,), (0,)), ((), ())), preferred_element_type=F32)


def widen(value, lanes):
    return jnp.concatenate(
        [value, jnp.zeros((value.shape[0], lanes - value.shape[1]), value.dtype)], axis=1
    )


def activation(gate, up, hidden_slope):
    square = gate * gate
    bent = jnp.tanh(ROOT * gate * (1.0 + 0.044715 * square))
    half = 0.5 * (1.0 + bent)
    value = gate * half
    slope = half + 0.5 * gate * (1.0 - bent * bent) * (ROOT * (1.0 + 3.0 * 0.044715 * square))
    return (
        (value * up).astype(BF16),
        (hidden_slope * up * slope).astype(BF16),
        (hidden_slope * value).astype(BF16),
    )


def layer_kernel(
    n_blk,
    n_dp,
    lengths,
    bucket_table,
    first_gain,
    second_gain,
    bias_table,
    tokens_hbm,
    cot_hbm,
    wq_hbm,
    wk_hbm,
    wv_hbm,
    wo_hbm,
    wg_hbm,
    wu_hbm,
    wd_hbm,
    mixed_out,
    tokgrad_out,
    small_out,
    attn_out,
    ff_out,
    tok_t,
    cot_t,
    tok,
    wq,
    wk,
    wv,
    wo,
    k_all,
    v_all,
    q_all,
    s_all,
    totals,
    deltas,
    probs,
    dq_rows,
    gat,
    streams,
    held_w,
    slopes,
    middle,
    mixed_acc,
    second_acc,
    attended,
    swap_out,
    swap_in,
    ff_part,
    ff_r1,
    ff_r2,
    rows,
    acol,
    grads_t,
    at_part,
    at_first,
    at_recv,
    ag,
    small,
    small_blk,
    small_dp,
    tables,
    onehot,
    diag,
    lay,
    load_sem,
    stream_sem,
    swap_sem,
    k_send,
    k_recv,
    v_send,
    v_recv,
    q_send,
    q_recv,
    s_send,
    s_recv,
    lt_send,
    lt_recv,
    de_send,
    de_recv,
    gat_send,
    gat_recv,
    row_send,
    row_recv,
    col_send,
    col_recv,
    ff_send,
    ff_sem,
    at_send,
    at_sem,
    ag_send,
    ag_sem,
    sb_send,
    sb_sem,
    sd_send,
    sd_sem,
):
    n_lo = n_blk // HI
    local, width = tok.shape
    lanes = rows.shape[2]
    inner = wq.shape[1]
    pairs = inner // LANES
    heads = 2 * pairs
    keys = n_blk * local
    ff = wg_hbm.shape[1]
    chunk = streams.shape[3]
    slots = streams.shape[1]
    half_ff = ff // 2
    n_chunk = half_ff // chunk
    cut = ff // (n_blk * n_dp)
    n_near = HI // 2
    last_dp = n_dp - 1

    blk = lax.axis_index("blk")
    dp = lax.axis_index("dp")
    hi, lo = blk // n_lo, blk % n_lo
    row_y, core = dp // 2, dp % 2
    z_far, z_near = hi // 2, hi % 2
    own = z_far * 4 + dp

    def push(src, dst, send, recv, to_blk, to_dp):
        return pltpu.make_async_remote_copy(
            src_ref=src,
            dst_ref=dst,
            send_sem=send,
            recv_sem=recv,
            device_id={"blk": to_blk, "dp": to_dp},
            device_id_type=pl.DeviceIdType.MESH,
        )

    loads = [
        pltpu.make_async_copy(src, dst, load_sem.at[i])
        for i, (src, dst) in enumerate(
            (
                (tokens_hbm, tok_t),
                (wk_hbm, wk),
                (wv_hbm, wv),
                (wq_hbm, wq),
                (cot_hbm, cot_t),
                (wo_hbm, wo),
            )
        )
    ]
    for load in loads:
        load.start()
    feeds = (wg_hbm, wu_hbm, wd_hbm)
    wide = chunk
    picks = []
    def piece_begin(q):
        xl, zn = q // n_near, q % n_near
        column = (((z_far * n_near + zn) * n_lo + xl) * n_dp + dp) * cut
        return column, jnp.minimum(column // LANES * LANES, ff - wide)

    for q in range(n_lo * n_near):
        start = pl.multiple_of(piece_begin(q)[1], LANES)
        for i, src in enumerate(feeds):
            picks.append(
                pltpu.make_async_copy(
                    src.at[:, pl.ds(start, wide)], streams.at[i, q], stream_sem.at[i, q]
                )
            )
    barrier = pltpu.get_barrier_semaphore()
    partners = [((blk + o) % n_blk, dp) for o in range(1, n_blk)]
    partners += [(blk, (dp + o) % n_dp) for o in range(1, n_dp)]
    for to_blk, to_dp in partners:
        pl.semaphore_signal(
            barrier,
            inc=1,
            device_id={"blk": to_blk, "dp": to_dp},
            device_id_type=pl.DeviceIdType.MESH,
        )

    z_other, near_other, lo_other = 1 - z_far, 1 - z_near, 1 - lo

    def place(zf, zn, xl):
        return (zf * n_near + zn) * n_lo + xl

    class Gather:
        def __init__(self, buf, send, recv):
            self.buf, self.send, self.recv = buf, send, recv

        def one(self, k, slot, to_blk):
            ref = self.buf.at[slot]
            return push(ref, ref, self.send.at[k], self.recv.at[k], to_blk, dp)

        def far(self):
            return self.one(0, blk, place(z_other, z_near, lo))

        def near(self, a):
            slot = place(z_other if a else z_far, z_near, lo)
            return self.one(1 + a, slot, place(z_far, near_other, lo))

        def low(self, a, b):
            slot = place(z_other if a else z_far, near_other if b else z_near, lo)
            return self.one(3 + 2 * a + b, slot, place(z_far, z_near, lo_other))

        def start(self):
            self.far().start()
            self.near(0).start()
            self.low(0, 0).start()

        def step_near(self):
            self.near(0).wait_recv()
            self.low(0, 1).start()

        def step_far(self):
            self.far().wait_recv()
            self.near(1).start()
            self.low(1, 0).start()

        def step_last(self):
            self.near(1).wait_recv()
            self.low(1, 1).start()

        def finish(self):
            for a in range(2):
                for b in range(2):
                    self.low(a, b).wait_recv()

        def drain(self):
            self.far().wait_send()
            for a in range(2):
                self.near(a).wait_send()
                for b in range(2):
                    self.low(a, b).wait_send()

    k_ring = Gather(k_all, k_send, k_recv)
    v_ring = Gather(v_all, v_send, v_recv)
    q_ring = Gather(q_all, q_send, q_recv)
    s_ring = Gather(s_all, s_send, s_recv)

    eye = (
        lax.broadcasted_iota(jnp.int32, (local, local), 0)
        == lax.broadcasted_iota(jnp.int32, (local, local), 1)
    ).astype(BF16)
    gain1 = first_gain[...].astype(F32).reshape(1, width)
    gain2 = second_gain[...].astype(F32).reshape(1, width)
    loads[0].wait()
    x = nt(eye, tok_t[...])
    tok[...] = x.astype(BF16)
    first_scale = lax.rsqrt(jnp.mean(x * x, axis=-1, keepdims=True) + EPS)
    normed = (x * first_scale * gain1).astype(BF16)
    rows[dp] = widen(normed, lanes)
    loads[1].wait()
    for load in picks:
        load.start()
    k_all[blk] = nn(normed, wk[...]).astype(BF16)
    pl.semaphore_wait(barrier, len(partners))
    k_ring.start()
    loads[2].wait()
    v_all[blk] = nn(normed, wv[...]).astype(BF16)
    v_ring.start()

    y_other, core_other = 1 - row_y, 1 - core

    def row_push(k, slot, to, src=None):
        src = rows.at[slot] if src is None else src
        return push(src, rows.at[slot], row_send.at[k], row_recv.at[k], blk, to)

    other_dp = row_y * 2 + core_other

    def row_across():
        return row_push(0, dp, other_dp)

    def row_down():
        return row_push(1, dp, core)

    def row_on():
        return row_push(2, 2 + core, core_other)

    def row_up(src=None):
        return row_push(3 + core, dp, 2, src)

    def row_across_last():
        return row_push(7, dp, last_dp, brow)

    def row_last(src):
        return row_push(5 + core, dp, last_dp, src)

    lower = row_y == 0
    last = dp == last_dp

    def to_dp(o, who):
        return (dp + o) % n_dp == who

    pl.when(dp != 2)(lambda: row_across().start())
    pl.when(jnp.logical_not(lower))(lambda: row_down().start())

    loads[3].wait()
    q_all[blk] = nn(normed, wq[...]).astype(BF16)
    loads[4].wait()
    gat[1, own] = widen(nt(eye, cot_t[...]).astype(BF16), lanes)


    def gat_push(which, k, slot, to_blk, to_dp, at=slice(None)):
        ref = gat.at[which, slot, at]
        return push(ref, ref, gat_send.at[which, k], gat_recv.at[which, k], to_blk, to_dp)

    parts = [pl.ds(0, local // 2), pl.ds(local // 2, local // 2)]

    def gat_z(which, part):
        to = (z_other * n_near + z_near) * n_lo + lo
        return gat_push(which, part, own, to, dp, parts[part])

    def gat_y(which):
        return gat_push(which, 2, own, blk, y_other * 2 + core)

    def gat_y_far(which, part):
        slot = z_other * 4 + dp
        return gat_push(which, 3 + part, slot, blk, y_other * 2 + core, parts[part])

    def gat_core(which, a, b):
        slot = (z_far + a) % 2 * 4 + (row_y + b) % 2 * 2 + core
        return gat_push(which, 5 + a * 2 + b, slot, blk, row_y * 2 + core_other)

    def gat_far(which):
        for part in range(2):
            gat_z(which, part).start()

    def gat_start(which):
        gat_y(which).start()
        gat_core(which, 0, 0).start()

    def gat_forward(which, part):
        gat_z(which, part).wait_recv()
        gat_y_far(which, part).start()
        if part:
            gat_core(which, 1, 0).start()

    def gat_across(which, a):
        if a:
            for part in range(2):
                gat_y_far(which, part).wait_recv()
        else:
            gat_y(which).wait_recv()
        gat_core(which, a, 1).start()

    gat_start(1)
    r = lax.broadcasted_iota(jnp.int32, (cut, wide), 0)
    c = lax.broadcasted_iota(jnp.int32, (cut, wide), 1)
    for load in picks:
        load.wait()
    def pick_piece(k, carry):
        q, i = k // 3, k % 3
        column, start = piece_begin(q)
        pick = jnp.where(c - r == column - start, 1.0, 0.0).astype(BF16)
        piece = nt(pick, streams[i, q]).astype(BF16)
        held_w[i, pl.ds(pl.multiple_of(q * cut, 16), cut), :] = widen(piece, lanes)
        return carry

    lax.fori_loop(0, 3 * n_lo * n_near, pick_piece, 0)

    def stream(i, c):
        begin = pl.multiple_of(core * half_ff + c * chunk, chunk)
        slot = c % slots
        return pltpu.make_async_copy(
            feeds[i].at[:, pl.ds(begin, chunk)], streams.at[i, slot], stream_sem.at[i, slot]
        )

    def stream_next(i, c):
        pl.when(c + slots < n_chunk)(lambda: stream(i, c + slots).start())

    for c in range(slots):
        for i in (2, 0, 1):
            stream(i, c).start()
    k_ring.step_near()
    v_ring.step_near()

    near_span = 4 * local
    lane_near = lax.broadcasted_iota(jnp.int32, (8, near_span), 1)
    n_table = bucket_table.shape[0]
    n_bucket = bias_table.shape[1]
    held_lanes = 3 * LANES
    bucket = jnp.concatenate(
        [
            bucket_table[...].astype(F32).reshape(1, n_table),
            jnp.zeros((1, held_lanes - n_table), F32),
        ],
        axis=1,
    )
    bucket = jnp.broadcast_to(bucket, (8, held_lanes))
    turn = (
        lax.broadcasted_iota(jnp.int32, (held_lanes, held_lanes), 0)
        + lax.broadcasted_iota(jnp.int32, (held_lanes, held_lanes), 1)
        == n_table - 1
    ).astype(BF16)

    def bias_rows(line):
        line = jnp.concatenate([line, jnp.zeros((8, near_span - held_lanes), F32)], axis=1)
        line = jnp.where(lane_near >= n_table, line[:, n_table - 1 : n_table], line)
        moved = pltpu.roll(line, local - 1, 1)
        moved = jnp.where(lane_near < local - 1, line[:, 0:1], moved)
        hot = (
            jnp.broadcast_to(moved[0:1], (n_bucket, near_span))
            == lax.broadcasted_iota(jnp.int32, (n_bucket, near_span), 0).astype(F32)
        ).astype(F32)
        return hot, nn(bias_table[...], hot.astype(BF16))

    hots, tables[0] = bias_rows(bucket)
    onehot[...] = hots
    tables[1] = bias_rows(nn(bucket.astype(BF16), turn))[1]
    here_pos = blk * local + lax.broadcasted_iota(jnp.int32, (local, 1), 0)
    pack_pos = lax.broadcasted_iota(jnp.int32, (1, keys), 1)
    here_item = jnp.zeros((local, 1), jnp.int32)
    pack_item = jnp.zeros((1, keys), jnp.int32)
    end = jnp.int32(0)
    for m in range(lengths.shape[1]):
        end = end + lengths[0, m]
        here_item += (here_pos >= end).astype(jnp.int32)
        pack_item += (pack_pos >= end).astype(jnp.int32)

    near_at = pl.multiple_of(blk * local, local)
    inside = slice(local, local + keys)
    lane_lay = lax.broadcasted_iota(jnp.int32, (1, lay.shape[1]), 1)

    def bias_tile(turned, h):
        line = tables[turned, pl.ds(h, 1), :]
        ends_row = jnp.where(lane_lay < near_at, line[:, 0:1], line[:, near_span - 1 : near_span])
        lay[...] = jnp.broadcast_to(ends_row, lay.shape)
        rolled = pltpu.roll(
            jnp.broadcast_to(line, (local, near_span)), 1, 1, stride=1, stride_axis=0
        )
        lay[:, pl.ds(near_at, 3 * local)] = rolled[:, local:]
        return jnp.where(here_item == pack_item, lay[:, inside], -1e30)

    def fill_bias(h, carry):
        probs[h] = bias_tile(0, h)
        return carry

    lax.fori_loop(0, heads, fill_bias, 0)

    k_ring.step_far()
    gat_far(1)

    both = pl.ds((z_far * n_near + row_y) * 2, 2)
    gat_core(1, 0, 0).wait_recv()

    def hidden_slopes(c, carry):
        stream(2, c).wait()
        rows_c = gat[1, both].reshape(2 * local, lanes)[:, 0:width]
        slopes[c] = nn(rows_c, streams[2, c % slots]).astype(BF16)
        stream_next(2, c)
        return carry

    third = n_chunk // 3
    lax.fori_loop(0, third, hidden_slopes, 0)
    k_ring.step_last()
    v_ring.step_far()
    lax.fori_loop(third, n_chunk, hidden_slopes, 0)
    for c in range(slots):
        stream(2, c).start()
    k_ring.finish()

    @pl.when(lower)
    def _():
        row_down().wait_recv()
        row_on().start()

    lane = lax.broadcasted_iota(jnp.int32, (local, LANES), 1)
    low_half = lane < LANES // 2

    def halves(block):
        zero = jnp.zeros_like(block)
        return jnp.concatenate(
            [jnp.where(low_half, block, zero), jnp.where(low_half, zero, block)], axis=0
        )

    def joined(both):
        return jnp.where(low_half, both[0:local], both[local:])

    def pair_at(p):
        return pl.ds(pl.multiple_of(p * LANES, LANES), LANES)

    def cols_of(ref, p):
        return ref[:, :, pair_at(p)].reshape(keys, LANES)

    def softmax(p, stat):
        raw = nt(halves(q_all[blk, :, pair_at(p)]), cols_of(k_all, p))
        for s in range(2):
            h = 2 * p + s
            score = raw[s * local : (s + 1) * local] + probs[h]
            high = jnp.max(score, axis=-1, keepdims=True)
            expo = jnp.exp(score - high)
            total = jnp.sum(expo, axis=-1, keepdims=True)
            probs[h] = expo * (1.0 / total)
            stat = jnp.where(lane == h, high + jnp.log(total), stat)
        pl.when(p == 0)(v_ring.step_last)
        return stat

    stat = lax.fori_loop(0, pairs, softmax, jnp.zeros((local, LANES), F32))
    mine_at = pl.ds(pl.multiple_of(blk * local, local), local)

    def line_push(buf, send, recv, o):
        mine = buf.at[:, mine_at]
        return push(mine, mine, send.at[o], recv.at[o], (blk + o) % n_blk, dp)

    def total_push(o):
        return line_push(totals, lt_send, lt_recv, o)

    def delta_push(o):
        return line_push(deltas, de_send, de_recv, o)

    q_ring.start()
    totals[:, mine_at] = stat.T[0:8]
    for o in range(1, n_blk):
        total_push(o).start()
    v_ring.finish()

    def attend(p, carry):
        low = probs[pl.ds(2 * p, 2)].reshape(2 * local, keys).astype(BF16)
        attended[:, pair_at(p)] = joined(nn(low, cols_of(v_all, p)))
        return carry

    lax.fori_loop(0, pairs, attend, 0)

    gat_forward(1, 0)
    gat_forward(1, 1)
    gat_across(1, 0)
    loads[5].wait()
    attention = attended[...].astype(BF16)
    mid = tok[...].astype(F32) + nt(attention, wo[...])
    middle[...] = mid
    second_scale = lax.rsqrt(jnp.mean(mid * mid, axis=-1, keepdims=True) + EPS)
    gat[0, own] = widen((mid * second_scale * gain2).astype(BF16), lanes)
    gat_far(0)
    gat_start(0)

    grads_t[3] = attended[...].T.astype(BF16)

    mixed_acc[...] = jnp.zeros_like(mixed_acc)
    second_acc[...] = jnp.zeros_like(second_acc)
    gat_core(0, 0, 0).wait_recv()

    def feed(c, carry):
        slot = c % slots
        for i in range(3):
            stream(i, c).wait()
        normed2 = gat[0, both].reshape(2 * local, lanes)[:, 0:width]
        gate = nn(normed2, streams[0, slot])
        up = nn(normed2, streams[1, slot])
        hidden, gate_slope, up_slope = activation(gate, up, slopes[c].astype(F32))
        mixed_acc[...] += nt(hidden, streams[2, slot]).reshape(mixed_acc.shape)
        total = nt(gate_slope, streams[0, slot]) + nt(up_slope, streams[1, slot])
        second_acc[...] += total.reshape(second_acc.shape)
        for i in range(3):
            stream_next(i, c)
        return carry

    half = n_chunk // 2
    lax.fori_loop(0, half, feed, 0)
    q_ring.step_near()
    q_ring.step_far()
    gat_across(1, 1)
    lax.fori_loop(half, n_chunk - 1, feed, 0)
    gat_across(0, 0)
    q_ring.step_last()
    lax.fori_loop(n_chunk - 1, n_chunk, feed, 0)

    def swap_push(k):
        return push(
            swap_out.at[k], swap_in.at[k], swap_sem.at[k], swap_sem.at[2 + k], blk, other_dp
        )

    swap_out[0] = widen(second_acc[core_other].astype(BF16), lanes)
    swap_push(0).start()
    swap_out[1] = widen(mixed_acc[core_other].astype(BF16), lanes)
    swap_push(1).start()
    gat_forward(0, 0)
    swap_push(0).wait_recv()

    mid = middle[...]
    second_scale = lax.rsqrt(jnp.mean(mid * mid, axis=-1, keepdims=True) + EPS)
    second_slope = second_acc[core] + swap_in[0, :, 0:width].astype(F32)
    small[...] = jnp.zeros_like(small)
    quarter = lanes // 4

    def small_line(first_row, line):
        line = widen(line, lanes)
        for q in range(4):
            at = slice(q * quarter, (q + 1) * quarter)
            small[first_row + q : first_row + q + 1, 0:quarter] = line[:, at]

    small_line(4, jnp.sum(second_slope * mid * second_scale, axis=0, keepdims=True))
    scaled = second_slope * gain2
    middle_slope = (
        gat[1, own, :, 0:width].astype(F32)
        + second_scale * scaled
        - mid
        * (second_scale * second_scale * second_scale)
        * jnp.mean(scaled * mid, axis=-1, keepdims=True)
    )
    mixed_acc[core] = mid + mixed_acc[core]
    middle[...] = middle_slope
    branch = middle_slope.astype(BF16)
    s_all[blk] = nn(branch, wo[...]).astype(BF16)
    s_ring.start()
    product = s_all[blk].astype(F32) * attended[...]
    delta_cols = jnp.zeros((local, LANES), F32)
    for h in range(heads):
        piece = product[:, (h // 2) * LANES : (h // 2 + 1) * LANES]
        mine = low_half if h % 2 == 0 else jnp.logical_not(low_half)
        delta = jnp.sum(jnp.where(mine, piece, 0.0), axis=-1, keepdims=True)
        delta_cols = jnp.where(lane == h, delta, delta_cols)
    deltas[:, mine_at] = delta_cols.T[0:8]
    for o in range(1, n_blk):
        delta_push(o).start()

    swap_push(0).wait_send()
    brow = swap_out.at[0]
    brow[...] = widen(branch, lanes)

    @pl.when(last)
    def _():
        row_across().wait_send()
        row_down().wait_send()
        rows[dp] = widen(branch, lanes)

    def col_push(o):
        to = (dp + o) % n_dp
        begin = pl.multiple_of(dp * local, local)
        return push(
            grads_t.at[to],
            acol.at[:, pl.ds(begin, local)],
            col_send.at[o],
            col_recv.at[o],
            blk,
            to,
        )


    step = 2 * local
    held = held_w.shape[1]

    def recompute(k, carry):
        a, b = k // 2, k % 2

        @pl.when(k > 0)
        def _():
            for which in range(2):
                gat_core(which, a, b).wait_recv()

        t = (z_far + a) % 2 * n_near + (row_y + b) % 2
        rows_n = gat[0, pl.ds(2 * t, 2)].reshape(step, lanes)
        rows_c = gat[1, pl.ds(2 * t, 2)].reshape(step, lanes)
        gate = nt(held_w[0], rows_n)
        up = nt(held_w[1], rows_n)
        hidden_slope = nt(held_w[2], rows_c)
        hidden, gate_slope, up_slope = activation(gate, up, hidden_slope)
        streams[0, t, 0:held, :] = gate_slope
        streams[1, t, 0:held, :] = up_slope
        streams[2, t, 0:held, :] = hidden
        return carry

    lax.fori_loop(0, 1, recompute, 0)
    gat_forward(0, 1)
    s_ring.step_near()
    pl.when(lower)(lambda: row_last(brow).start())
    pl.when(dp == 2)(lambda: row_across_last().start())

    flip = (
        lax.broadcasted_iota(jnp.int32, (local, local), 0)
        + lax.broadcasted_iota(jnp.int32, (local, local), 1)
        == local - 1
    ).astype(BF16)
    diag[...] = jnp.zeros_like(diag)
    lay[...] = jnp.zeros_like(lay)
    def query_side(p, carry):
        dots = nt(halves(s_all[blk, :, pair_at(p)]), cols_of(v_all, p))
        ds = []
        for s in range(2):
            h = 2 * p + s
            delta = jnp.sum(jnp.where(lane == h, delta_cols, 0.0), axis=-1, keepdims=True)
            one = (probs[h] * (dots[s * local : (s + 1) * local] - delta)).astype(BF16)
            wide_one = one.astype(F32)
            lay[:, inside] = wide_one
            near = lay[:, pl.ds(near_at, 3 * local)].astype(BF16)
            padded = jnp.concatenate([nn(flip, near), jnp.zeros((local, local), F32)], axis=1)
            skewed = pltpu.roll(padded, 0, 1, stride=1, stride_axis=0)
            total = jnp.sum(wide_one, axis=0, keepdims=True)
            before = jnp.sum(jnp.where(pack_pos < near_at - local, total, 0.0), axis=1, keepdims=True)
            after = jnp.sum(
                jnp.where(pack_pos >= near_at + 2 * local, total, 0.0), axis=1, keepdims=True
            )
            line = jnp.sum(skewed, axis=0, keepdims=True)
            line = line + jnp.where(lane_near[0:1] == 0, before, 0.0)
            diag[pl.ds(h, 1), :] = line + jnp.where(lane_near[0:1] == near_span - 1, after, 0.0)
            ds.append(one)
        dq = joined(nn(jnp.concatenate(ds, axis=0), cols_of(k_all, p)))
        dq_rows[:, pair_at(p)] = dq.astype(BF16)
        grads_t[0, pair_at(p), :] = dq.T.astype(BF16)
        return carry

    lax.fori_loop(0, pairs, query_side, 0)
    for o in range(1, n_dp):
        pl.when(jnp.logical_or(to_dp(o, 0), to_dp(o, last_dp)))(lambda o=o: col_push(o).start())
    pl.when(lower)(lambda: row_up().start())
    s_ring.step_far()
    gat_across(0, 1)
    lax.fori_loop(1, 2, recompute, 0)

    s_ring.step_last()
    lax.fori_loop(2, HI, recompute, 0)

    lo_far, near_far = 1 - lo, 1 - z_near
    along_lo_blk = hi * n_lo + lo_far
    along_z_blk = (z_far * n_near + near_far) * n_lo + lo

    def split():
        return slice(0, 48), slice(48, cut)

    def ff_hop(src, dst, w, k, to_blk):
        return push(src, dst, ff_send.at[w, k], ff_sem.at[w, k], to_blk, dp)

    def ff_hop1(w):
        by_lo, by_z = split()
        return (
            ff_hop(ff_part.at[w, lo_far, :, by_lo], ff_r1.at[w, :, by_lo], w, 0, along_lo_blk),
            ff_hop(ff_part.at[w, :, near_far, by_z], ff_r1.at[w, :, by_z], w, 1, along_z_blk),
        )

    def ff_hop2(w):
        by_lo, by_z = split()
        return (
            ff_hop(ff_part.at[w, lo, near_far, by_lo], ff_r2.at[w, by_lo], w, 2, along_z_blk),
            ff_hop(ff_part.at[w, lo_far, z_near, by_z], ff_r2.at[w, by_z], w, 3, along_lo_blk),
        )

    def ff_middle(w):
        by_lo, by_z = split()
        one, two = ff_hop1(w)
        far, near = ff_hop2(w)
        one.wait_recv()
        ff_part[w, lo, near_far, by_lo] = (
            ff_part[w, lo, near_far, by_lo].astype(F32) + ff_r1[w, near_far, by_lo].astype(F32)
        ).astype(BF16)
        far.start()
        two.wait_recv()
        ff_part[w, lo_far, z_near, by_z] = (
            ff_part[w, lo_far, z_near, by_z].astype(F32) + ff_r1[w, lo_far, by_z].astype(F32)
        ).astype(BF16)
        near.start()

    def ff_last(w):
        by_lo, by_z = split()
        far, near = ff_hop2(w)
        far.wait_recv()
        near.wait_recv()
        mine = ff_part[w, lo, z_near].astype(F32) + ff_r2[w].astype(F32)
        ff_out[w, by_lo] = mine[by_lo] + ff_r1[w, z_near, by_lo].astype(F32)
        ff_out[w, by_z] = mine[by_z] + ff_r1[w, lo, by_z].astype(F32)

    def at_hop1():
        to = hi * n_lo + 1 - lo
        return push(at_part.at[1 - lo], at_first, at_send.at[0], at_sem.at[0], to, dp)

    def at_hop2(o):
        to = (hi + o) % HI
        return push(
            at_part.at[lo, to], at_recv.at[hi], at_send.at[o], at_sem.at[o], to * n_lo + lo, dp
        )

    def attention_gradient():
        acol[:, pl.ds(pl.multiple_of(dp * local, local), local)] = grads_t[dp]

        @pl.when(lower)
        def _():
            row_across().wait_recv()
            row_on().wait_recv()

        @pl.when(dp == 2)
        def _():
            row_across().wait_recv()
            for k in (3, 4):
                row_push(k, dp, 2).wait_recv()

        @pl.when(last)
        def _():
            for k in (5, 6, 7):
                row_push(k, dp, last_dp).wait_recv()

        for o in range(1, n_dp):
            col_push(o).wait_recv()
        total = nn(acol[...], rows[...].reshape(n_dp * local, lanes))
        total = total.astype(BF16).reshape(n_blk, inner // n_blk, lanes)
        for b in range(n_blk):
            at_part[b % n_lo, b // n_lo] = total[b]
        at_hop1().start()

    def attention_gradient_next():
        at_hop1().wait_recv()
        at_part[lo] = (at_part[lo].astype(F32) + at_first[...].astype(F32)).astype(BF16)
        for o in range(1, HI):
            at_hop2(o).start()
        at_recv[hi] = at_part[lo, hi]

    early = jnp.logical_or(dp == 0, dp == last_dp)

    order = (2, 0, 1)

    def gradient(k, carry):
        w = (k + 2) % 3
        left = jnp.concatenate([streams[w, t, 0:held, :] for t in range(HI)], axis=1)
        total = nn(left, gat[w // 2].reshape(2 * HI * local, lanes))
        ff_part[w] = total.astype(BF16).reshape(n_lo, n_near, cut, lanes)
        for hop in ff_hop1(w):
            hop.start()
        return carry

    pl.when(early)(attention_gradient)
    lax.fori_loop(0, 1, gradient, 0)

    q_ring.finish()
    for o in range(1, n_blk):
        total_push(o).wait_recv()

    def key_weights(p, carry):
        raw = nt(halves(k_all[blk, :, pair_at(p)]), cols_of(q_all, p))
        for s in range(2):
            h = 2 * p + s
            piece = slice(s * local, (s + 1) * local)
            probs[h] = jnp.exp(raw[piece] + bias_tile(1, h) - totals[pl.ds(h, 1), :])
        return carry

    lax.fori_loop(0, pairs, key_weights, 0)


    s_ring.finish()
    for o in range(1, n_blk):
        delta_push(o).wait_recv()

    def key_side(p, carry):
        queries = cols_of(q_all, p)
        slopes_p = cols_of(s_all, p)
        dots = nt(halves(v_all[blk, :, pair_at(p)]), slopes_p)
        low = []
        ds = []
        for s in range(2):
            h = 2 * p + s
            prob = probs[h]
            low.append(prob.astype(BF16))
            dot = dots[s * local : (s + 1) * local]
            ds.append((prob * (dot - deltas[pl.ds(h, 1), :])).astype(BF16))
        dk = joined(nn(jnp.concatenate(ds, axis=0), queries))
        dv = joined(nn(jnp.concatenate(low, axis=0), slopes_p))
        grads_t[1, pair_at(p), :] = dk.T.astype(BF16)
        grads_t[2, pair_at(p), :] = dv.T.astype(BF16)
        return carry

    lax.fori_loop(0, pairs, key_side, 0)
    for o in range(1, n_dp):
        middle_two = jnp.logical_or(to_dp(o, 1), to_dp(o, 2))
        pl.when(middle_two)(lambda o=o: col_push(o).start())

    lax.fori_loop(1, 2, gradient, 0)
    ff_middle(order[0])
    bias_grad = lax.dot_general(
        diag[...],
        onehot[...],
        (((1,), (1,)), ((), ())),
        precision=lax.Precision.HIGHEST,
        preferred_element_type=F32,
    )
    small[0:heads, quarter : quarter + n_bucket] = bias_grad[0:heads]

    pl.when(jnp.logical_not(early))(attention_gradient)
    lax.fori_loop(2, 3, gradient, 0)

    x = tok[...].astype(F32)
    first_scale = lax.rsqrt(jnp.mean(x * x, axis=-1, keepdims=True) + EPS)
    key_slope = grads_t[1].astype(F32).T.astype(BF16)
    value_slope = grads_t[2].astype(F32).T.astype(BF16)
    first_slope = nt(dq_rows[...], wq[...]) + nt(key_slope, wk[...]) + nt(value_slope, wv[...])
    small_line(0, jnp.sum(first_slope * x * first_scale, axis=0, keepdims=True))

    def small_blk_push(o):
        return push(small, small_blk.at[blk], sb_send.at[o], sb_sem.at[o], (blk + o) % n_blk, dp)

    for o in range(1, n_blk):
        small_blk_push(o).start()
    small_blk[blk] = small[...]
    scaled = first_slope * gain1
    token_slope = (
        middle[...]
        + first_scale * scaled
        - x
        * (first_scale * first_scale * first_scale)
        * jnp.mean(scaled * x, axis=-1, keepdims=True)
    )
    tokgrad_out[...] = token_slope.T

    ff_middle(order[1])
    attention_gradient_next()
    for o in range(1, n_blk):
        small_blk_push(o).wait_recv()
    total = small_blk[0]
    for b in range(1, n_blk):
        total += small_blk[b]
    small_dp[dp] = total

    def small_dp_push(o):
        return push(
            small_dp.at[dp], small_dp.at[dp], sd_send.at[o], sd_sem.at[o], blk, (dp + o) % n_dp
        )

    for o in range(1, n_dp):
        small_dp_push(o).start()

    ff_middle(order[2])
    swap_push(1).wait_recv()
    mixed = mixed_acc[core] + swap_in[1, :, 0:width].astype(F32)
    mixed_out[...] = mixed.T.astype(BF16)
    for o in range(1, HI):
        at_hop2(o).wait_recv()
    total = at_recv[0].astype(F32)
    for b in range(1, HI):
        total += at_recv[b].astype(F32)
    ag[dp] = total.astype(BF16)

    def ag_push(o):
        return push(ag.at[dp], ag.at[dp], ag_send.at[o], ag_sem.at[o], blk, (dp + o) % n_dp)

    for o in range(1, n_dp):
        ag_push(o).start()
    for w in order:
        ff_last(w)

    for o in range(1, n_dp):
        small_dp_push(o).wait_recv()
        ag_push(o).wait_recv()
    total = small_dp[0]
    for d in range(1, n_dp):
        total += small_dp[d]
    small_out[...] = jnp.zeros_like(small_out)
    for q in range(4):
        at = slice(q * quarter, (q + 1) * quarter)
        small_out[0:1, at] = total[q : q + 1, 0:quarter]
        small_out[1:2, at] = total[4 + q : 5 + q, 0:quarter]
    small_out[2 : 2 + heads, 0:n_bucket] = total[0:heads, quarter : quarter + n_bucket]
    for a in range(4):
        attn_out[a] = ag[a].astype(F32)

    for ring in (k_ring, v_ring, q_ring, s_ring):
        ring.drain()
    for which in range(2):
        gat_y(which).wait_send()
        for a in range(2):
            gat_z(which, a).wait_send()
            gat_y_far(which, a).wait_send()
            for b in range(2):
                gat_core(which, a, b).wait_send()

    @pl.when(lower)
    def _():
        row_across().wait_send()
        row_on().wait_send()
        row_up().wait_send()
        row_last(brow).wait_send()

    @pl.when(dp == 2)
    def _():
        row_down().wait_send()
        row_across_last().wait_send()

    for o in range(1, n_dp):
        col_push(o).wait_send()
        small_dp_push(o).wait_send()
        ag_push(o).wait_send()
    for o in range(1, n_blk):
        total_push(o).wait_send()
        delta_push(o).wait_send()
        small_blk_push(o).wait_send()
    swap_push(1).wait_send()
    at_hop1().wait_send()
    for o in range(1, HI):
        at_hop2(o).wait_send()
    for w in order:
        for hop in ff_hop1(w) + ff_hop2(w):
            hop.wait_send()


def spread_kernel(small, mixed, tokens_gradient, attn, ff_grads, *outs):
    gain1, gain2, bias, mixed_out, tokens_out = outs[:5]
    width = gain1.shape[0]
    gain1[...] = small[0, 0:width]
    gain2[...] = small[1, 0:width]
    bias[...] = small[2 : 2 + bias.shape[0], 0 : bias.shape[1]]
    mixed_out[...] = mixed[...]
    tokens_out[...] = tokens_gradient[...]
    for a in range(4):
        outs[5 + a][...] = attn[a, :, 0:width]
    for w in range(3):
        outs[9 + w][...] = ff_grads[w, :, 0:width]


def fused(
    n_blk,
    n_dp,
    tokens,
    lengths,
    bucket_table,
    first_gain,
    position_bias,
    w_query,
    w_key,
    w_value,
    w_output,
    second_gain,
    w_gate,
    w_up,
    w_down,
    cotangent,
):
    local, width = tokens.shape[1:]
    inner = w_query.shape[1]
    ff = w_gate.shape[1]
    n_bucket, heads = position_bias.shape
    keys = n_blk * local
    cut = ff // (n_blk * n_dp)
    n_lo = n_blk // HI
    held = n_lo * (HI // 2) * cut
    part = inner // n_blk
    pairs = inner // LANES
    chunk = 256
    lanes = -(-width // LANES) * LANES
    dma, vmem = pltpu.SemaphoreType.DMA, pltpu.VMEM
    any_spec = pl.BlockSpec(memory_space=pl.ANY)
    vmem_spec = pl.BlockSpec(memory_space=pltpu.VMEM)
    smem_spec = pl.BlockSpec(memory_space=pltpu.SMEM)
    scratch = [
        vmem((width, local), BF16),
        vmem((width, local), BF16),
        vmem((local, width), BF16),
        vmem((width, inner), BF16),
        vmem((width, inner), BF16),
        vmem((width, inner), BF16),
        vmem((width, inner), BF16),
        vmem((n_blk, local, inner), BF16),
        vmem((n_blk, local, inner), BF16),
        vmem((n_blk, local, inner), BF16),
        vmem((n_blk, local, inner), BF16),
        vmem((8, keys), F32),
        vmem((8, keys), F32),
        vmem((2 * pairs, local, keys), F32),
        vmem((local, inner), BF16),
        vmem((2, 2 * HI, local, lanes), BF16),
        vmem((3, 4, width, chunk), BF16),
        vmem((3, held, lanes), BF16),
        vmem((ff // 2 // chunk, 2 * local, chunk), BF16),
        vmem((local, width), F32),
        vmem((2, local, width), F32),
        vmem((2, local, width), F32),
        vmem((local, inner), F32),
        vmem((2, local, lanes), BF16),
        vmem((2, local, lanes), BF16),
        vmem((3, n_lo, HI // 2, cut, lanes), BF16),
        vmem((3, 2, cut, lanes), BF16),
        vmem((3, cut, lanes), BF16),
        vmem((n_dp, local, lanes), BF16),
        vmem((inner, n_dp * local), BF16),
        vmem((4, inner, local), BF16),
        vmem((n_lo, HI, part, lanes), BF16),
        vmem((HI, part, lanes), BF16),
        vmem((HI, part, lanes), BF16),
        vmem((n_dp, part, lanes), BF16),
        vmem((8, lanes // 4 + LANES), F32),
        vmem((n_blk, 8, lanes // 4 + LANES), F32),
        vmem((n_dp, 8, lanes // 4 + LANES), F32),
        vmem((2, heads + heads % 2, 4 * local), F32),
        vmem((n_bucket, 4 * local), F32),
        vmem((8, 4 * local), F32),
        vmem((local, keys + 2 * local), F32),
        dma((6,)),
        dma((3, 4)),
        dma((4,)),
    ]
    for shape in (
        (7,),
        (7,),
        (7,),
        (7,),
        (n_blk,),
        (n_blk,),
        (2, 9),
        (8,),
        (n_dp,),
        (3, 4),
        (HI,),
        (n_dp,),
        (n_blk,),
        (n_dp,),
    ):
        scratch += [dma(shape), dma(shape)]
    mixed, tokens_gradient, small, attn, ff_grads = pl.pallas_call(
        functools.partial(layer_kernel, n_blk, n_dp),
        out_shape=(
            jax.ShapeDtypeStruct((width, local), BF16),
            jax.ShapeDtypeStruct((width, local), F32),
            jax.ShapeDtypeStruct((8, lanes), F32),
            jax.ShapeDtypeStruct((4, part, lanes), F32),
            jax.ShapeDtypeStruct((3, cut, lanes), F32),
        ),
        in_specs=[smem_spec] + [vmem_spec] * 4 + [any_spec] * 9,
        out_specs=(vmem_spec,) * 5,
        scratch_shapes=scratch,
        compiler_params=pltpu.CompilerParams(
            collective_id=0, has_side_effects=True, vmem_limit_bytes=64 * 1024 * 1024 - 65536
        ),
    )(
        lengths,
        bucket_table,
        first_gain,
        second_gain,
        position_bias.T,
        tokens[0].T,
        cotangent[0].T,
        w_query,
        w_key,
        w_value,
        w_output.T,
        w_gate,
        w_up,
        w_down.T,
    )
    outs = pl.pallas_call(
        spread_kernel,
        out_shape=[
            jax.ShapeDtypeStruct((width,), F32),
            jax.ShapeDtypeStruct((width,), F32),
            jax.ShapeDtypeStruct((heads, n_bucket), F32),
            jax.ShapeDtypeStruct((width, local), BF16),
            jax.ShapeDtypeStruct((width, local), F32),
        ]
        + [jax.ShapeDtypeStruct((part, width), F32)] * 4
        + [jax.ShapeDtypeStruct((cut, width), F32)] * 3,
        in_specs=[vmem_spec] * 5,
        out_specs=[vmem_spec] * 12,
    )(small, mixed, tokens_gradient, attn, ff_grads)
    gain1, gain2, bias, mixed, tokens_gradient, query, key, value, output, gate, up, down = outs
    return (
        mixed.T[None],
        tokens_gradient.T[None],
        gain1,
        bias.T,
        query.T,
        key.T,
        value.T,
        output,
        gain2,
        gate.T,
        up.T,
        down,
    )


def normalize(values, gain):
    return values * lax.rsqrt(jnp.mean(values * values, axis=-1, keepdims=True) + 1e-06) * gain


def gelu_tanh(values):
    return (
        0.5
        * values
        * (
            1.0
            + jnp.tanh(math.sqrt(2.0 / math.pi) * (values + 0.044715 * values * values * values))
        )
    )


def activate(gate, up_part):
    return gelu_tanh(gate) * up_part


def blocked(block_fn, carry, piece):
    count = piece[0].shape[0]
    size = 512
    parts = tuple((arr.reshape((count // size, size) + arr.shape[1:]) for arr in piece))

    def visit(state, inputs):
        number, block = inputs
        return (block_fn(state, block, number * size), None)

    state, _ = lax.scan(visit, carry, (jnp.arange(count // size, dtype=jnp.int32), parts))
    return state


def diagonal_sums(slope, shift, reach, table_len):
    heads, rows, cols = slope.shape
    width = rows + cols
    flipped = slope[:, ::-1, :]
    padded = jnp.pad(flipped, ((0, 0), (0, 0), (0, rows)))
    skewed = padded.reshape(heads, rows * width)[:, : rows * (width - 1)].reshape(
        heads, rows, width - 1
    )
    diagonal = jnp.sum(skewed, axis=1)
    relative = shift + jnp.arange(width - 1, dtype=jnp.int32) - (rows - 1)
    index = jnp.clip(relative, -reach, reach) + reach
    selector = (index[:, None] == jnp.arange(table_len, dtype=jnp.int32)[None, :]).astype(
        jnp.float32
    )
    return jnp.dot(
        diagonal, selector, precision=lax.Precision.HIGHEST, preferred_element_type=jnp.float32
    )


def on_device(
    tokens,
    lengths,
    bucket_table,
    first_gain,
    position_bias,
    w_query,
    w_key,
    w_value,
    w_output,
    second_gain,
    w_gate,
    w_up,
    w_down,
    cotangent,
):
    f32 = jnp.float32
    bf16 = jnp.bfloat16
    heads = position_bias.shape[1]
    inner = w_query.shape[1]
    head_size = inner // heads
    local = tokens.shape[1]
    table_len = bucket_table.shape[0]
    reach = (table_len - 1) // 2
    inputs = tokens[0].astype(f32)
    positions = lax.axis_index("blk") * local + jnp.arange(local, dtype=jnp.int32)
    ends = jnp.cumsum(lengths[0])
    onehot = (
        bucket_table[:, None] == jnp.arange(position_bias.shape[0], dtype=jnp.int32)[None, :]
    ).astype(f32)
    head_rows = jnp.einsum(
        "rb,bh->hr", onehot, position_bias.astype(f32), precision=lax.Precision.HIGHEST
    )

    def item_of(places):
        return jnp.sum((places[:, None] >= ends[None, :]).astype(jnp.int32), axis=1)

    def pair_scores(query3, key3, query_pos, key_pos):
        offset = jnp.clip(key_pos[None, :] - query_pos[:, None], -reach, reach) + reach
        raw = jnp.einsum("qhd,khd->hqk", query3, key3, preferred_element_type=f32) + jnp.take(
            head_rows, offset, axis=1
        )
        mask = item_of(query_pos)[:, None] == item_of(key_pos)[None, :]
        return (jnp.where(mask[None], raw, -1e30), mask)

    normed_first, first_back = jax.vjp(normalize, inputs, first_gain.astype(f32))
    normed_first_low = normed_first.astype(bf16)
    queries = jnp.dot(normed_first_low, w_query, preferred_element_type=f32).astype(bf16)
    keys_low = jnp.dot(normed_first_low, w_key, preferred_element_type=f32).astype(bf16)
    values_low = jnp.dot(normed_first_low, w_value, preferred_element_type=f32).astype(bf16)
    query3 = queries.reshape(local, heads, head_size)
    key3_own = keys_low.reshape(local, heads, head_size)
    value3_own = values_low.reshape(local, heads, head_size)

    def forward_block(state, piece, start):
        high, total, running = state
        key_piece, value_piece = piece
        count = key_piece.shape[0]
        key_pos = start + jnp.arange(count, dtype=jnp.int32)
        scores, mask = pair_scores(
            query3, key_piece.reshape(count, heads, head_size), positions, key_pos
        )
        new_high = jnp.maximum(high, jnp.max(scores, axis=-1))
        weights = jnp.where(mask[None], jnp.exp(scores - new_high[..., None]), 0.0)
        factor = jnp.exp(high - new_high)
        total = total * factor + jnp.sum(weights, axis=-1)
        running = running * factor.T[:, :, None] + jnp.einsum(
            "hqk,khd->qhd",
            weights.astype(bf16),
            value_piece.reshape(count, heads, head_size),
            preferred_element_type=f32,
        )
        return (new_high, total, running)

    start_state = (
        jnp.full((heads, local), -1e30, f32),
        jnp.zeros((heads, local), f32),
        jnp.zeros((local, heads, head_size), f32),
    )
    high, total, running = blocked(
        forward_block,
        start_state,
        (
            lax.all_gather(keys_low, "blk", axis=0, tiled=True),
            lax.all_gather(values_low, "blk", axis=0, tiled=True),
        ),
    )
    log_total = high + jnp.log(total)
    attended = running / total.T[:, :, None]
    attention = attended.reshape(local, inner).astype(bf16)
    middle = inputs + jnp.dot(attention, w_output, preferred_element_type=f32)
    normed_second, second_back = jax.vjp(normalize, middle, second_gain.astype(f32))
    normed_second_low = normed_second.astype(bf16)
    gate = jnp.dot(normed_second_low, w_gate, preferred_element_type=f32)
    up_part = jnp.dot(normed_second_low, w_up, preferred_element_type=f32)
    hidden, activate_back = jax.vjp(activate, gate, up_part)
    hidden_low = hidden.astype(bf16)
    mixed = (middle + jnp.dot(hidden_low, w_down, preferred_element_type=f32)).astype(bf16)
    upstream = cotangent[0]
    down_local = jnp.einsum("td,tf->df", upstream, hidden_low, preferred_element_type=f32)
    hidden_slope = jnp.einsum("td,fd->tf", upstream, w_down, preferred_element_type=f32)
    gate_raw, up_raw = activate_back(hidden_slope)
    gate_slope = gate_raw.astype(bf16)
    up_slope = up_raw.astype(bf16)
    gate_local = jnp.einsum("td,tf->df", normed_second_low, gate_slope, preferred_element_type=f32)
    up_local = jnp.einsum("td,tf->df", normed_second_low, up_slope, preferred_element_type=f32)
    second_slope = jnp.einsum(
        "tf,df->td", gate_slope, w_gate, preferred_element_type=f32
    ) + jnp.einsum("tf,df->td", up_slope, w_up, preferred_element_type=f32)
    middle_norm_slope, second_gain_local = second_back(second_slope)
    middle_slope = upstream.astype(f32) + middle_norm_slope
    feed_parts = None
    branch_slope = middle_slope.astype(bf16)
    output_local = jnp.einsum("td,ti->di", branch_slope, attention, preferred_element_type=f32)
    attention_slope = jnp.einsum(
        "td,id->ti", branch_slope, w_output, preferred_element_type=f32
    ).astype(bf16)
    slope3 = attention_slope.reshape(local, heads, head_size)
    delta_rows = jnp.sum(slope3.astype(f32) * attended, axis=-1)
    delta_heads = delta_rows.T

    def query_block(state, piece, start):
        query_acc, table_acc = state
        key_piece, value_piece = piece
        count = key_piece.shape[0]
        key_pos = start + jnp.arange(count, dtype=jnp.int32)
        key3 = key_piece.reshape(count, heads, head_size)
        scores, mask = pair_scores(query3, key3, positions, key_pos)
        weights = jnp.where(mask[None], jnp.exp(scores - log_total[..., None]), 0.0)
        value_dots = jnp.einsum(
            "qhd,khd->hqk",
            slope3,
            value_piece.reshape(count, heads, head_size),
            preferred_element_type=f32,
        )
        score_slope = (weights * (value_dots - delta_heads[..., None])).astype(bf16)
        query_acc = query_acc + jnp.einsum(
            "hqk,khd->qhd", score_slope, key3, preferred_element_type=f32
        )
        table_acc = table_acc + diagonal_sums(
            score_slope.astype(f32), start - positions[0], reach, table_len
        )
        return (query_acc, table_acc)

    query_init = (jnp.zeros((local, heads, head_size), f32), jnp.zeros((heads, table_len), f32))
    query_acc, table_acc = blocked(
        query_block,
        query_init,
        (
            lax.all_gather(keys_low, "blk", axis=0, tiled=True),
            lax.all_gather(values_low, "blk", axis=0, tiled=True),
        ),
    )
    whole_total, whole_delta = (
        lax.all_gather(log_total.T, "blk", axis=0, tiled=True),
        lax.all_gather(delta_rows, "blk", axis=0, tiled=True),
    )

    def key_block(state, piece, start):
        key_acc, value_acc = state
        query_piece, slope_piece = piece
        count = query_piece.shape[0]
        query_pos = start + jnp.arange(count, dtype=jnp.int32)
        query3p = query_piece.reshape(count, heads, head_size)
        slope3p = slope_piece.reshape(count, heads, head_size)
        scores, mask = pair_scores(query3p, key3_own, query_pos, positions)
        piece_total = lax.dynamic_slice_in_dim(whole_total, start, count, 0).T
        piece_delta = lax.dynamic_slice_in_dim(whole_delta, start, count, 0).T
        weights = jnp.where(mask[None], jnp.exp(scores - piece_total[..., None]), 0.0)
        value_dots = jnp.einsum("qhd,khd->hqk", slope3p, value3_own, preferred_element_type=f32)
        score_slope = (weights * (value_dots - piece_delta[..., None])).astype(bf16)
        key_acc = key_acc + jnp.einsum(
            "hqk,qhd->khd", score_slope, query3p, preferred_element_type=f32
        )
        value_acc = value_acc + jnp.einsum(
            "hqk,qhd->khd", weights.astype(bf16), slope3p, preferred_element_type=f32
        )
        return (key_acc, value_acc)

    key_init = (
        jnp.zeros((local, heads, head_size), f32),
        jnp.zeros((local, heads, head_size), f32),
    )
    key_acc, value_acc = blocked(
        key_block,
        key_init,
        (
            lax.all_gather(queries, "blk", axis=0, tiled=True),
            lax.all_gather(attention_slope, "blk", axis=0, tiled=True),
        ),
    )
    query_slope = query_acc.reshape(local, inner).astype(bf16)
    key_slope = key_acc.reshape(local, inner).astype(bf16)
    value_slope = value_acc.reshape(local, inner).astype(bf16)
    query_local = jnp.einsum("td,ti->di", normed_first_low, query_slope, preferred_element_type=f32)
    key_local = jnp.einsum("td,ti->di", normed_first_low, key_slope, preferred_element_type=f32)
    value_local = jnp.einsum("td,ti->di", normed_first_low, value_slope, preferred_element_type=f32)
    first_slope = (
        jnp.einsum("ti,di->td", query_slope, w_query, preferred_element_type=f32)
        + jnp.einsum("ti,di->td", key_slope, w_key, preferred_element_type=f32)
        + jnp.einsum("ti,di->td", value_slope, w_value, preferred_element_type=f32)
    )
    input_norm_slope, first_gain_local = first_back(first_slope)
    tokens_gradient = middle_slope + input_norm_slope
    bias_local = jnp.einsum("rb,hr->bh", onehot, table_acc, precision=lax.Precision.HIGHEST)
    feed_parts = (
        lax.psum_scatter(gate_local, ("blk", "dp"), scatter_dimension=1, tiled=True),
        lax.psum_scatter(up_local, ("blk", "dp"), scatter_dimension=1, tiled=True),
        lax.psum_scatter(down_local, ("blk", "dp"), scatter_dimension=1, tiled=True),
    )
    attention_parts = (
        lax.psum_scatter(
            query_local.astype(jnp.bfloat16), "blk", scatter_dimension=1, tiled=True
        ).astype(jnp.float32),
        lax.psum_scatter(
            key_local.astype(jnp.bfloat16), "blk", scatter_dimension=1, tiled=True
        ).astype(jnp.float32),
        lax.psum_scatter(
            value_local.astype(jnp.bfloat16), "blk", scatter_dimension=1, tiled=True
        ).astype(jnp.float32),
        lax.psum_scatter(
            output_local.astype(jnp.bfloat16), "blk", scatter_dimension=1, tiled=True
        ).astype(jnp.float32),
    )
    attention_parts = (
        lax.psum(attention_parts[0].astype(jnp.bfloat16), "dp").astype(jnp.float32),
        lax.psum(attention_parts[1].astype(jnp.bfloat16), "dp").astype(jnp.float32),
        lax.psum(attention_parts[2].astype(jnp.bfloat16), "dp").astype(jnp.float32),
        lax.psum(attention_parts[3].astype(jnp.bfloat16), "dp").astype(jnp.float32),
    )
    first_total, bias_total, second_total = lax.psum(
        (first_gain_local, bias_local, second_gain_local), ("blk", "dp")
    )
    return (
        mixed[None],
        tokens_gradient[None],
        first_total,
        bias_total,
        attention_parts[0],
        attention_parts[1],
        attention_parts[2],
        attention_parts[3].T,
        second_total,
        feed_parts[0],
        feed_parts[1],
        feed_parts[2].T,
    )


def solution(mesh):
    n_blk, n_dp = mesh.shape["blk"], mesh.shape["dp"]

    def on_any(*args):
        local = args[0].shape[1]
        inner, ff = args[5].shape[1], args[10].shape[1]
        fits = n_blk * local <= 1024 and n_dp == 4 and n_blk == 2 * HI
        if fits and ff % (16 * n_blk * n_dp) == 0 and inner % (16 * n_blk) == 0:
            return fused(n_blk, n_dp, *args)
        return on_device(*args)

    return jax.shard_map(
        on_any,
        mesh=mesh,
        in_specs=(
            P("dp", "blk", None),
            P("dp", None),
            P(),
            P(),
            P(),
            P(),
            P(),
            P(),
            P(),
            P(),
            P(),
            P(),
            P(),
            P("dp", "blk", None),
        ),
        out_specs=(
            P("dp", "blk", None),
            P("dp", "blk", None),
            P(),
            P(),
            P(None, "blk"),
            P(None, "blk"),
            P(None, "blk"),
            P("blk", None),
            P(),
            P(None, ("blk", "dp")),
            P(None, ("blk", "dp")),
            P(("blk", "dp"), None),
        ),
        check_vma=False,
    )
```
